32 devices in a mesh: blk: 8 (over z, y), dir: 4 (over x, core).
Axes of the slice: x: 2, y: 2, z: 4, core: 2. Of those that a mesh axis runs over, the one named last changes fastest.
Arguments:
- sky_map: float32 [4, 128, 8192], P('dir', 'blk'), may hold values from -6 to 6
- order_ids: int32 [32], replicated, may hold values from 0 to 4063, as said below
- legendre: float32 [32, 64, 128], P('blk'), may hold values from -0.5 to 0.5
- wigner: float32 [4, 32, 64, 128], P('dir', 'blk'), may hold values from -0.125 to 0.125
- wavelet: float32 [4, 64], P('dir'), may hold values from 0.5 to 1.5
- dir_ids: int32 [4], replicated, may hold values from 0 to 3, each once
Outputs:
- modulus: float32 [4, 4, 128, 8192], P('dir', None, 'blk')
The draws below stay inside these ranges and needn't reach their ends.
Inputs may be any that keep to these rules, and one draw needn't show every extreme that they name: `order_ids`: distinct orders; the 4 slots of each index of blk hold pairs: its first 2 slots hold m values, its last 2 slots hold 4063 - m for the same m in order. `dir_ids`: a permutation.
All inputs are finite; a program needn't handle non-finite values.
Results may differ from the reference program's by a relative error of at most 0.0001.
Values sent between devices are 32-bit elements; how exact they have to be, the bound alone decides.
A program may use at most 64 MiB of HBM per device.

```python
import math
import jax
import jax.numpy as jnp
from jax import lax

L = 4096
NPHI = 8192
NN = 4
NDEG = 64
M_DEV = 4
NTHETA = 128
SLAB = 32
MAPS = 4
N_BLK = 8


def draw_order_ids(key, part):
    key = jax.random.fold_in(key, 7)
    order_limit = L - NDEG // 2
    halves = order_limit // 2
    picked = jax.random.permutation(key, halves - 1)[:SLAB // 2 - 1] + 1
    lower_half = jnp.concatenate([jnp.zeros((1,), jnp.int32), picked.astype(jnp.int32)])
    lower_half = jax.random.permutation(jax.random.fold_in(key, 1), lower_half)
    upper_half = order_limit - 1 - lower_half
    paired = jnp.concatenate([lower_half.reshape(N_BLK, M_DEV // 2), upper_half.reshape(N_BLK, M_DEV // 2)], axis=1)
    return paired.reshape(SLAB).astype(jnp.int32)


def level_of(key, extent, split, smallest, high):
    factor_of = 1.0
    for dim, blocks in split:
        steps = jax.random.uniform(jax.random.fold_in(jax.random.fold_in(key, 6), dim), (blocks,), jnp.float32, smallest / len(split), high / len(split))
        factor_of = factor_of * jnp.repeat(jnp.exp(steps), extent[dim] // blocks).reshape((-1,) + (1,) * (len(extent) - 1 - dim))
    return factor_of


def bell_draw(key, extent, deviation, bound, pieces=(), kind=jnp.bfloat16):
    factor_of = level_of(key, extent, pieces, -0.22, 0.18) if pieces else 1.0
    array = jax.random.normal(key, extent, jnp.float32) * deviation * factor_of
    return jnp.minimum(jnp.maximum(array, -bound), bound).astype(kind)


def setup_inputs(seed: int = 0) -> dict:
    splits = jax.random.split(jax.random.key(seed), 7)
    return {
        "sky_map": bell_draw(splits[0], (MAPS, NTHETA, NPHI), 1.0, 6.0, ((0, 4), (1, 8)), jnp.float32),
        "order_ids": draw_order_ids(jax.random.fold_in(splits[6], 71), 0),
        "legendre": bell_draw(splits[2], (SLAB, NDEG, NTHETA), NTHETA ** -0.5, 0.5, ((0, 8),), jnp.float32),
        "wigner": bell_draw(splits[3], (NN, SLAB, NDEG, NTHETA), (NDEG * SLAB) ** -0.5, 0.125, ((0, 4), (1, 8)), jnp.float32),
        "wavelet": jnp.clip(0.5 + 1.0 * jax.random.uniform(splits[4], (NN, NDEG), jnp.float32) ** level_of(splits[4], (NN, NDEG), ((0, 4),), -0.2, 0.2), 0.5, 1.5),
        "dir_ids": jax.random.permutation(splits[5], NN).astype(jnp.int32),
    }


HIGHEST_PRECISION = lax.Precision.HIGHEST

def order_tables(order_ids, longitudes):
    column = jnp.arange(longitudes, dtype=jnp.int32)
    phase = column[:, None] * order_ids[None, :].astype(jnp.int32) % longitudes
    angles = phase.astype(jnp.float32) * (2.0 * math.pi / longitudes)
    return (jnp.cos(angles), jnp.sin(angles))

def reference(sky_map, order_ids, legendre, wigner, wavelet, dir_ids):
    cosine, sine_table = order_tables(order_ids, NPHI)
    factor = 1.0 / math.sqrt(NPHI)
    spec_real = jnp.einsum('ptk,ks->pts', sky_map, cosine, precision=HIGHEST_PRECISION) * factor
    spec_imag = -jnp.einsum('ptk,ks->pts', sky_map, sine_table, precision=HIGHEST_PRECISION) * factor
    degree = L - NDEG + jnp.arange(NDEG, dtype=jnp.int32)
    live_mask = (degree[None, :] >= order_ids[:, None].astype(jnp.int32)).astype(jnp.float32)
    coeff_real = jnp.einsum('slt,pts->psl', legendre, spec_real, precision=HIGHEST_PRECISION) * live_mask
    coeff_imag = jnp.einsum('slt,pts->psl', legendre, spec_imag, precision=HIGHEST_PRECISION) * live_mask
    parts_real = []
    parts_imag = []
    for component in range(NN):
        parts_real.append(jnp.einsum('slt,psl->pts', wigner[component], coeff_real * wavelet[component], precision=HIGHEST_PRECISION))
        parts_imag.append(jnp.einsum('slt,psl->pts', wigner[component], coeff_imag * wavelet[component], precision=HIGHEST_PRECISION))
    comp_real = jnp.stack(parts_real)
    comp_imag = jnp.stack(parts_imag)
    azimuths = (2 * jnp.arange(NN, dtype=jnp.int32) - NN + 1).astype(jnp.float32)

    def one_direction(direction):
        angle_dir = math.pi * direction.astype(jnp.float32) / NN
        cos_mix = jnp.cos(azimuths * angle_dir)
        sin_mix = jnp.sin(azimuths * angle_dir)
        mixed_real = jnp.einsum('i,ipts->pts', cos_mix, comp_real, precision=HIGHEST_PRECISION) - jnp.einsum('i,ipts->pts', sin_mix, comp_imag, precision=HIGHEST_PRECISION)
        mixed_imag = jnp.einsum('i,ipts->pts', sin_mix, comp_real, precision=HIGHEST_PRECISION) + jnp.einsum('i,ipts->pts', cos_mix, comp_imag, precision=HIGHEST_PRECISION)
        map_real = jnp.einsum('pts,ks->ptk', mixed_real, cosine, precision=HIGHEST_PRECISION) - jnp.einsum('pts,ks->ptk', mixed_imag, sine_table, precision=HIGHEST_PRECISION)
        map_imag = jnp.einsum('pts,ks->ptk', mixed_real, sine_table, precision=HIGHEST_PRECISION) + jnp.einsum('pts,ks->ptk', mixed_imag, cosine, precision=HIGHEST_PRECISION)
        return jnp.sqrt(map_real * map_real + map_imag * map_imag)
    return lax.map(one_direction, dir_ids)
```

```python
import functools
import math

import jax
import jax.numpy as jnp
from jax import lax
from jax.experimental import pallas as pl
from jax.experimental.pallas import tpu as pltpu
from jax.sharding import PartitionSpec as P

L = 4096
INNER = 512
LANES = 128
MESH = pl.DeviceIdType.MESH


def sin_turn(phase, turn):
    quarter = turn // 4
    shifted = lax.bitwise_and(phase + quarter, turn - 1)
    folded = quarter - jnp.abs(shifted - 2 * quarter)
    u = folded.astype(jnp.float32) * (1.0 / quarter)
    square = u * u
    half = math.pi / 2
    total = jnp.full_like(u, -(half**11) / math.factorial(11))
    for power in (9, 7, 5, 3, 1):
        sign = 1.0 if power % 4 == 1 else -1.0
        total = total * square + sign * half**power / math.factorial(power)
    return total * u


def halves(value):
    high = value.astype(jnp.bfloat16)
    low = (value - high.astype(jnp.float32)).astype(jnp.bfloat16)
    return high, low


def iota(shape, dim):
    return lax.broadcasted_iota(jnp.int32, shape, dim)


def column_of(scalars, row, rows_of):
    value = jnp.full(row.shape, scalars[0], jnp.int32)
    for index in range(1, len(scalars)):
        value = jnp.where(rows_of(row) == index, scalars[index], value)
    return value


def dot(a, b, dims):
    return lax.dot_general(a, b, (dims, ((), ())), preferred_element_type=jnp.float32)


def spectra_kernel(
    blks, dirs, order_ref, dir_ref, sky_ref, legendre_ref, wigner_ref, wavelet_ref,
    mixed_ref, send1, recv1, send2, recv2, send_sem, recv_sem,
):
    blk, own = lax.axis_index("blk"), lax.axis_index("dir")
    devices = blks * dirs
    own_slot = own * blks + blk
    cycles, turn = sky_ref.shape[1], sky_ref.shape[2]
    orders, degrees, thetas = legendre_ref.shape
    steps = turn // INNER
    groups = LANES // cycles
    maps = dirs

    barrier = pltpu.get_barrier_semaphore()

    def greet(step, carry):
        other = lax.rem(own_slot + step, devices)
        pl.semaphore_signal(
            barrier, inc=1, device_id=(lax.rem(other, blks), lax.div(other, blks)),
            device_id_type=MESH,
        )
        return carry

    lax.fori_loop(1, devices, greet, 0)

    pieces = [sky_ref[0, :, a * INNER:(a + 1) * INNER] for a in range(steps)]
    sky_high, sky_low = halves(jnp.concatenate(pieces, axis=0))
    sky_both = jnp.concatenate([sky_high, sky_low], axis=0)
    rows = 2 * orders
    width = steps * cycles
    tile_row = iota((rows, LANES), 0)
    lane = iota((rows, LANES), 1)
    scale = 1.0 / math.sqrt(turn)

    def spectrum(group, carry):
        ids = []
        for j in range(groups):
            base = (group * groups + j) * orders
            ids.append(column_of(
                [order_ref[base + s] for s in range(orders)], tile_row,
                lambda r: lax.rem(r, orders),
            ))
        column = jnp.concatenate(ids, axis=0)
        tall = groups * rows
        part = lax.rem(lax.div(iota((tall, LANES), 0), orders), 2)
        offset = (1 + part) * (turn // 4)
        position = iota((tall, LANES), 1)
        table = jnp.concatenate(
            [sin_turn(column * (position + LANES * c) + offset, turn) for c in range(INNER // LANES)],
            axis=1,
        )
        table_high, table_low = halves(table)
        product = dot(jnp.concatenate([table_high, table_low], axis=0), sky_both, ((1,), (1,)))
        inner = product[:tall, :width] + product[:tall, width:] + product[tall:, :width]
        swapped = jnp.concatenate(
            [
                piece
                for j in range(groups)
                for piece in (
                    inner[j * rows + orders:(j + 1) * rows], inner[j * rows:j * rows + orders])
            ],
            axis=0,
        )
        total = jnp.zeros((tall, LANES), jnp.float32)
        for c in range(width // LANES):
            phase = column * (lax.div(position + LANES * c, cycles) * INNER)
            cut = slice(c * LANES, (c + 1) * LANES)
            total += sin_turn(phase + turn // 4, turn) * inner[:, cut]
            total += sin_turn(phase + part * (turn // 2), turn) * swapped[:, cut]
        shift = LANES // 2
        while shift >= cycles:
            total = total + pltpu.roll(total, shift, 1)
            shift //= 2
        total = total * scale
        for j in range(groups):
            block = jnp.where(lax.div(lane, cycles) == tile_row, total[j * rows:(j + 1) * rows], 0.0)
            send1[group * groups + j] = jnp.sum(block, axis=0, keepdims=True)
        return carry

    lax.fori_loop(0, blks // groups, spectrum, 0, unroll=blks == groups)

    pl.semaphore_wait(barrier, devices - 1)

    def scatter(send, recv, phase):
        def one(step, carry):
            other = lax.rem(own_slot + step, devices)
            other_blk, other_dir = lax.rem(other, blks), lax.div(other, blks)
            pltpu.make_async_remote_copy(
                src_ref=send.at[other_blk], dst_ref=recv.at[own_slot],
                send_sem=send_sem.at[phase], recv_sem=recv_sem.at[phase],
                device_id=(other_blk, other_dir), device_id_type=MESH,
            ).start()
            return carry

        lax.fori_loop(1, devices, one, 0)
        recv[own_slot] = send[blk]

    def settle(recv, sem, phase):
        span = recv.at[pl.ds(0, devices - 1)]
        pltpu.make_async_copy(span, span, sem.at[phase]).wait()

    scatter(send1, recv1, 0)

    flat = orders * degrees
    legendre_both = jnp.concatenate(halves(legendre_ref[...].reshape(flat, thetas)), axis=0)
    wigner_high, wigner_low = halves(wigner_ref[0].reshape(flat, thetas))
    tall = maps * rows
    own_ids = column_of(
        [order_ref[blk * orders + s] for s in range(orders)], iota((tall, flat), 0),
        lambda r: lax.rem(r, orders),
    )
    place = iota((tall, flat), 1)
    same = lax.div(place, degrees) == lax.rem(iota((tall, flat), 0), orders)
    live = L - degrees + lax.rem(place, degrees) >= own_ids
    weight = jnp.concatenate([wavelet_ref[...]] * orders, axis=1)
    weight = jnp.where(same & live, weight, 0.0)

    settle(recv1, recv_sem, 0)

    spectra = []
    for p in range(maps):
        chunks = []
        for g in range(blks // groups):
            start = p * blks + g * groups
            block = recv1[start:start + groups].reshape(groups, LANES)
            out = jnp.where(lax.div(lane, cycles) == tile_row, block, 0.0)
            for shift in range(1, groups):
                turned = pltpu.roll(pltpu.roll(block, groups - shift, 0), shift * cycles, 1)
                hit = lax.div(lane, cycles) == lax.rem(tile_row + shift, groups)
                out = jnp.where(hit, turned, out)
            chunks.append(out)
        spectra.append(jnp.concatenate(chunks, axis=1))
    both = jnp.concatenate(halves(jnp.concatenate(spectra, axis=0)), axis=0)
    product = dot(both, legendre_both, ((1,), (1,)))
    coeffs = product[:tall, :flat] + product[:tall, flat:] + product[tall:, :flat]
    both = jnp.concatenate(halves(coeffs * weight), axis=0)
    first = dot(both, wigner_high, ((1,), (0,)))
    second = dot(both[:tall], wigner_low, ((1,), (0,)))
    component = first[:tall] + first[tall:] + second

    for h in range(thetas // LANES):
        turned = [
            [
                block if shift == 0 else pltpu.roll(block, shift * cycles, 1)
                for shift in range(groups)
            ]
            for block in (
                component[p * rows:(p + 1) * rows, h * LANES:(h + 1) * LANES] for p in range(maps)
            )
        ]
        for j in range(groups):
            block = turned[0][(-j) % groups]
            for target in range(1, groups):
                block = jnp.where(
                    lax.div(lane, cycles) == target,
                    turned[target % maps][(target - j) % groups], block,
                )
            send2[h * groups + j] = jnp.where(
                lane[:orders] < LANES // 2, block[:orders], block[orders:]
            )

    scatter(send2, recv2, 1)

    direction = dir_ref[own]
    half_lane = iota((blks * orders, LANES), 1) < LANES // 2

    settle(recv2, recv_sem, 1)

    mixed = jnp.zeros((blks * orders, LANES), jnp.float32)
    for i in range(dirs):
        value = recv2[i * blks:(i + 1) * blks].reshape(blks * orders, LANES)
        azimuth = 2 * i - dirs + 1
        phase = jnp.full((1, LANES), direction, jnp.int32) * (azimuth * (turn // (2 * dirs)))
        phase = phase + 4 * turn
        sine = sin_turn(phase, turn)
        mixed += sin_turn(phase + turn // 4, turn) * value
        mixed += jnp.where(half_lane, -sine, sine) * pltpu.roll(value, LANES // 2, 1)
    mixed_ref[...] = mixed

    settle(recv1, send_sem, 0)
    settle(recv2, send_sem, 1)


def maps_kernel(turn, maps, cycles, order_ref, mixed_ref, out_ref, total):
    slab = 32
    steps = turn // INNER
    chunks = mixed_ref.shape[0] // slab
    row = iota((8, LANES), 0)
    lane = iota((slab, LANES), 1)
    real = lane < LANES // 2

    def maps_of(chunk, last):
        column = jnp.concatenate(
            [
                column_of(
                    [order_ref[chunk * slab + q * 8 + s] for s in range(8)], row, lambda r: r)
                for q in range(slab // 8)
            ],
            axis=0,
        )
        phases = [column * (lane + LANES * c) for c in range(INNER // LANES)]
        cosine = jnp.concatenate([sin_turn(x + turn // 4, turn) for x in phases], axis=1)
        sine = jnp.concatenate([sin_turn(x, turn) for x in phases], axis=1)
        table = jnp.concatenate(
            [
                jnp.concatenate([cosine, sine], axis=1),
                jnp.concatenate([-sine, cosine], axis=1),
            ],
            axis=0,
        )
        table_high, table_low = halves(table)
        right = jnp.concatenate([table_high, table_high, table_low], axis=0)
        turns = [mixed_ref[pl.ds(chunk * slab, slab), :]]
        while len(turns) < steps:
            phase = column * (INNER * len(turns))
            across = sin_turn(phase + turn // 4, turn)
            sine_a = sin_turn(phase, turn)
            sine_a = jnp.where(real, -sine_a, sine_a)
            turns = turns + [
                across * value + sine_a * pltpu.roll(value, LANES // 2, 1) for value in turns
            ]
        for pair in range(steps // 2):
            one, two = turns[2 * pair], turns[2 * pair + 1]
            left = jnp.concatenate(
                [
                    jnp.where(real, one, pltpu.roll(two, LANES // 2, 1)),
                    jnp.where(real, pltpu.roll(one, LANES // 2, 1), two),
                ],
                axis=0,
            )
            left_high, left_low = halves(left)
            left = jnp.concatenate([left_high, left_low, left_high], axis=0)
            value = dot(left, right, ((0,), (0,)))
            if chunks > 1:
                value = value + total[pair]
                total[pair] = value
            if last:
                real_part, imag_part = value[:, :INNER], value[:, INNER:]
                modulus = jnp.sqrt(real_part * real_part + imag_part * imag_part)
                half = maps * cycles
                for part in range(2):
                    a = 2 * pair + part
                    out_ref[0, :, :, a * INNER:(a + 1) * INNER] = modulus[
                        part * half:(part + 1) * half
                    ].reshape(maps, cycles, INNER)

    if chunks > 1:
        total[...] = jnp.zeros_like(total)

        def partial(chunk, carry):
            maps_of(chunk, False)
            return carry

        lax.fori_loop(0, chunks - 1, partial, 0)
    maps_of(chunks - 1, True)


def local(blks, dirs, sky_map, order_ids, legendre, wigner, wavelet, dir_ids):
    devices = blks * dirs
    cycles, turn = sky_map.shape[1:]
    orders = legendre.shape[0]
    vmem = pl.BlockSpec(memory_space=pltpu.VMEM)
    smem = pl.BlockSpec(memory_space=pltpu.SMEM)
    mixed = pl.pallas_call(
        functools.partial(spectra_kernel, blks, dirs),
        out_shape=jax.ShapeDtypeStruct((blks * orders, LANES), jnp.float32),
        in_specs=[smem, smem, vmem, vmem, vmem, vmem],
        out_specs=vmem,
        scratch_shapes=[
            pltpu.VMEM((blks, 1, LANES), jnp.float32),
            pltpu.VMEM((devices, 1, LANES), jnp.float32),
            pltpu.VMEM((blks, orders, LANES), jnp.float32),
            pltpu.VMEM((devices, orders, LANES), jnp.float32),
            pltpu.SemaphoreType.DMA((2,)),
            pltpu.SemaphoreType.DMA((2,)),
        ],
        compiler_params=pltpu.CompilerParams(
            collective_id=0, has_side_effects=True, vmem_limit_bytes=48 * 2**20
        ),
    )(order_ids, dir_ids, sky_map, legendre, wigner, wavelet)
    several = blks * orders > 32
    total_shape = (turn // INNER // 2, LANES, 2 * INNER) if several else (1, 8, LANES)
    return pl.pallas_call(
        functools.partial(maps_kernel, turn, dirs, cycles),
        out_shape=jax.ShapeDtypeStruct((1, dirs, cycles, turn), jnp.float32),
        in_specs=[smem, vmem],
        out_specs=vmem,
        scratch_shapes=[pltpu.VMEM(total_shape, jnp.float32)],
        compiler_params=pltpu.CompilerParams(vmem_limit_bytes=48 * 2**20),
    )(order_ids, mixed)


def solution(mesh):
    return jax.shard_map(
        functools.partial(local, mesh.shape["blk"], mesh.shape["dir"]),
        mesh=mesh,
        in_specs=(
            P("dir", "blk", None),
            P(),
            P("blk", None, None),
            P("dir", "blk", None, None),
            P("dir", None),
            P(),
        ),
        out_specs=P("dir", None, "blk", None),
        check_vma=False,
    )
```

```python
import functools
import math

import jax
import jax.numpy as jnp
from jax import lax
from jax.experimental import pallas as pl
from jax.experimental.pallas import tpu as pltpu
from jax.sharding import PartitionSpec as P

L = 4096
INNER = 512
LANES = 128
MESH = pl.DeviceIdType.MESH


def sin_turn(phase, turn):
    quarter = turn // 4
    shifted = lax.bitwise_and(phase + quarter, turn - 1)
    folded = quarter - jnp.abs(shifted - 2 * quarter)
    u = folded.astype(jnp.float32) * (1.0 / quarter)
    square = u * u
    half = math.pi / 2
    total = jnp.full_like(u, -(half**11) / math.factorial(11))
    for power in (9, 7, 5, 3, 1):
        sign = 1.0 if power % 4 == 1 else -1.0
        total = total * square + sign * half**power / math.factorial(power)
    return total * u


def halves(value):
    high = value.astype(jnp.bfloat16)
    low = (value - high.astype(jnp.float32)).astype(jnp.bfloat16)
    return high, low


def iota(shape, dim):
    return lax.broadcasted_iota(jnp.int32, shape, dim)


def column_of(scalars, row, rows_of):
    value = jnp.full(row.shape, scalars[0], jnp.int32)
    for index in range(1, len(scalars)):
        value = jnp.where(rows_of(row) == index, scalars[index], value)
    return value


def dot(a, b, dims):
    return lax.dot_general(a, b, (dims, ((), ())), preferred_element_type=jnp.float32)


def spectra_kernel(
    blks, dirs, order_hbm, dir_hbm, sky_hbm, legendre_hbm, wigner_hbm, wavelet_hbm,
    mixed_ref, column_ref, order_ref, dir_ref, sky_ref, legendre_ref, wigner_ref, wavelet_ref,
    send1, recv1, send2, recv2, in_sem, send_sem, recv_sem,
):
    loads = [
        pltpu.make_async_copy(source, target, in_sem.at[index])
        for index, (source, target) in enumerate((
            (order_hbm, order_ref), (sky_hbm, sky_ref), (dir_hbm, dir_ref),
            (legendre_hbm, legendre_ref), (wigner_hbm, wigner_ref), (wavelet_hbm, wavelet_ref),
        ))
    ]
    for load in loads:
        load.start()
    blk, own = lax.axis_index("blk"), lax.axis_index("dir")
    devices = blks * dirs
    own_slot = own * blks + blk
    cycles, turn = sky_ref.shape[1], sky_ref.shape[2]
    orders, degrees, thetas = legendre_ref.shape
    steps = turn // INNER
    groups = LANES // cycles
    maps = dirs

    barrier = pltpu.get_barrier_semaphore()

    def greet(step, carry):
        other = lax.rem(own_slot + step, devices)
        pl.semaphore_signal(
            barrier, inc=1, device_id=(lax.rem(other, blks), lax.div(other, blks)),
            device_id_type=MESH,
        )
        return carry

    lax.fori_loop(1, devices, greet, 0)

    loads[0].wait()
    loads[1].wait()
    pieces = [sky_ref[0, :, a * INNER:(a + 1) * INNER] for a in range(steps)]
    sky_high, sky_low = halves(jnp.concatenate(pieces, axis=0))
    sky_both = jnp.concatenate([sky_high, sky_low], axis=0)
    rows = 2 * orders
    width = steps * cycles
    tile_row = iota((rows, LANES), 0)
    lane = iota((rows, LANES), 1)
    scale = 1.0 / math.sqrt(turn)

    def spectrum(group, carry):
        ids = []
        for j in range(groups):
            base = (group * groups + j) * orders
            ids.append(column_of(
                [order_ref[base + s] for s in range(orders)], tile_row,
                lambda r: lax.rem(r, orders),
            ))
        column = jnp.concatenate(ids, axis=0)
        tall = groups * rows
        part = lax.rem(lax.div(iota((tall, LANES), 0), orders), 2)
        offset = (1 + part) * (turn // 4)
        position = iota((tall, LANES), 1)
        table = jnp.concatenate(
            [sin_turn(column * (position + LANES * c) + offset, turn) for c in range(INNER // LANES)],
            axis=1,
        )
        table_high, table_low = halves(table)
        product = dot(jnp.concatenate([table_high, table_low], axis=0), sky_both, ((1,), (1,)))
        inner = product[:tall, :width] + product[:tall, width:] + product[tall:, :width]
        swapped = jnp.concatenate(
            [
                piece
                for j in range(groups)
                for piece in (
                    inner[j * rows + orders:(j + 1) * rows], inner[j * rows:j * rows + orders])
            ],
            axis=0,
        )
        total = jnp.zeros((tall, LANES), jnp.float32)
        for c in range(width // LANES):
            phase = column * (lax.div(position + LANES * c, cycles) * INNER)
            cut = slice(c * LANES, (c + 1) * LANES)
            total += sin_turn(phase + turn // 4, turn) * inner[:, cut]
            total += sin_turn(phase + part * (turn // 2), turn) * swapped[:, cut]
        shift = LANES // 2
        while shift >= cycles:
            total = total + pltpu.roll(total, shift, 1)
            shift //= 2
        total = total * scale
        for j in range(groups):
            block = jnp.where(lax.div(lane, cycles) == tile_row, total[j * rows:(j + 1) * rows], 0.0)
            send1[group * groups + j] = jnp.sum(block, axis=0, keepdims=True)
        return carry

    lax.fori_loop(0, blks // groups, spectrum, 0, unroll=blks == groups)

    pl.semaphore_wait(barrier, devices - 1)

    def scatter(send, recv, phase):
        def one(step, carry):
            other = lax.rem(own_slot + step, devices)
            other_blk, other_dir = lax.rem(other, blks), lax.div(other, blks)
            pltpu.make_async_remote_copy(
                src_ref=send.at[other_blk], dst_ref=recv.at[own_slot],
                send_sem=send_sem.at[phase], recv_sem=recv_sem.at[phase],
                device_id=(other_blk, other_dir), device_id_type=MESH,
            ).start()
            return carry

        lax.fori_loop(1, devices, one, 0)
        recv[own_slot] = send[blk]

    def settle(recv, sem, phase):
        span = recv.at[pl.ds(0, devices - 1)]
        pltpu.make_async_copy(span, span, sem.at[phase]).wait()

    scatter(send1, recv1, 0)

    for load in loads[2:]:
        load.wait()
    flat = orders * degrees
    legendre_both = jnp.concatenate(halves(legendre_ref[...].reshape(flat, thetas)), axis=0)
    wigner_high, wigner_low = halves(wigner_ref[0].reshape(flat, thetas))
    tall = maps * rows
    own_ids = column_of(
        [order_ref[blk * orders + s] for s in range(orders)], iota((tall, flat), 0),
        lambda r: lax.rem(r, orders),
    )
    place = iota((tall, flat), 1)
    same = lax.div(place, degrees) == lax.rem(iota((tall, flat), 0), orders)
    live = L - degrees + lax.rem(place, degrees) >= own_ids
    weight = jnp.concatenate([wavelet_ref[...]] * orders, axis=1)
    weight = jnp.where(same & live, weight, 0.0)

    settle(recv1, recv_sem, 0)

    spectra = []
    for p in range(maps):
        chunks = []
        for g in range(blks // groups):
            start = p * blks + g * groups
            block = recv1[start:start + groups].reshape(groups, LANES)
            out = jnp.where(lax.div(lane, cycles) == tile_row, block, 0.0)
            for shift in range(1, groups):
                turned = pltpu.roll(pltpu.roll(block, groups - shift, 0), shift * cycles, 1)
                hit = lax.div(lane, cycles) == lax.rem(tile_row + shift, groups)
                out = jnp.where(hit, turned, out)
            chunks.append(out)
        spectra.append(jnp.concatenate(chunks, axis=1))
    both = jnp.concatenate(halves(jnp.concatenate(spectra, axis=0)), axis=0)
    product = dot(both, legendre_both, ((1,), (1,)))
    coeffs = product[:tall, :flat] + product[:tall, flat:] + product[tall:, :flat]
    both = jnp.concatenate(halves(coeffs * weight), axis=0)
    first = dot(both, wigner_high, ((1,), (0,)))
    second = dot(both[:tall], wigner_low, ((1,), (0,)))
    component = first[:tall] + first[tall:] + second

    for h in range(thetas // LANES):
        turned = [
            [
                block if shift == 0 else pltpu.roll(block, shift * cycles, 1)
                for shift in range(groups)
            ]
            for block in (
                component[p * rows:(p + 1) * rows, h * LANES:(h + 1) * LANES] for p in range(maps)
            )
        ]
        for j in range(groups):
            block = turned[0][(-j) % groups]
            for target in range(1, groups):
                block = jnp.where(
                    lax.div(lane, cycles) == target,
                    turned[target % maps][(target - j) % groups], block,
                )
            send2[h * groups + j] = jnp.where(
                lane[:orders] < LANES // 2, block[:orders], block[orders:]
            )

    scatter(send2, recv2, 1)

    def put_columns(chunk, carry):
        for q in range(groups * orders // 8):
            base = chunk * groups * orders + 8 * q
            column_ref[pl.ds(pl.multiple_of(base, 8), 8), :] = column_of(
                [order_ref[base + s] for s in range(8)], tile_row, lambda r: r)
        return carry

    lax.fori_loop(0, blks // groups, put_columns, 0, unroll=blks == groups)

    direction = dir_ref[own]
    half_lane = iota((blks * orders, LANES), 1) < LANES // 2

    settle(recv2, recv_sem, 1)

    mixed = jnp.zeros((blks * orders, LANES), jnp.float32)
    for i in range(dirs):
        value = recv2[i * blks:(i + 1) * blks].reshape(blks * orders, LANES)
        azimuth = 2 * i - dirs + 1
        phase = jnp.full((1, LANES), direction, jnp.int32) * (azimuth * (turn // (2 * dirs)))
        phase = phase + 4 * turn
        sine = sin_turn(phase, turn)
        mixed += sin_turn(phase + turn // 4, turn) * value
        mixed += jnp.where(half_lane, -sine, sine) * pltpu.roll(value, LANES // 2, 1)
    mixed_ref[...] = mixed

    settle(recv1, send_sem, 0)
    settle(recv2, send_sem, 1)


def maps_kernel(turn, maps, cycles, column_ref, mixed_ref, out_ref, total):
    slab = 32
    steps = turn // INNER
    chunks = mixed_ref.shape[0] // slab
    lane = iota((slab, LANES), 1)
    real = lane < LANES // 2

    def maps_of(chunk, last):
        column = column_ref[pl.ds(chunk * slab, slab), :]
        phases = [column * (lane + LANES * c) for c in range(INNER // LANES)]
        cosine = jnp.concatenate([sin_turn(x + turn // 4, turn) for x in phases], axis=1)
        sine = jnp.concatenate([sin_turn(x, turn) for x in phases], axis=1)
        table = jnp.concatenate(
            [
                jnp.concatenate([cosine, sine], axis=1),
                jnp.concatenate([-sine, cosine], axis=1),
            ],
            axis=0,
        )
        table_high, table_low = halves(table)
        right = jnp.concatenate([table_high, table_high, table_low], axis=0)
        turns = [mixed_ref[pl.ds(chunk * slab, slab), :]]
        while len(turns) < steps:
            phase = column * (INNER * len(turns))
            across = sin_turn(phase + turn // 4, turn)
            sine_a = sin_turn(phase, turn)
            sine_a = jnp.where(real, -sine_a, sine_a)
            turns = turns + [
                across * value + sine_a * pltpu.roll(value, LANES // 2, 1) for value in turns
            ]
        for pair in range(steps // 2):
            one, two = turns[2 * pair], turns[2 * pair + 1]
            left = jnp.concatenate(
                [
                    jnp.where(real, one, pltpu.roll(two, LANES // 2, 1)),
                    jnp.where(real, pltpu.roll(one, LANES // 2, 1), two),
                ],
                axis=0,
            )
            left_high, left_low = halves(left)
            left = jnp.concatenate([left_high, left_low, left_high], axis=0)
            value = dot(left, right, ((0,), (0,)))
            if chunks > 1:
                value = value + total[pair]
                total[pair] = value
            if last:
                real_part, imag_part = value[:, :INNER], value[:, INNER:]
                modulus = jnp.sqrt(real_part * real_part + imag_part * imag_part)
                half = maps * cycles
                for part in range(2):
                    a = 2 * pair + part
                    out_ref[0, :, :, a * INNER:(a + 1) * INNER] = modulus[
                        part * half:(part + 1) * half
                    ].reshape(maps, cycles, INNER)

    if chunks > 1:
        total[...] = jnp.zeros_like(total)

        def partial(chunk, carry):
            maps_of(chunk, False)
            return carry

        lax.fori_loop(0, chunks - 1, partial, 0)
    maps_of(chunks - 1, True)


def local(blks, dirs, sky_map, order_ids, legendre, wigner, wavelet, dir_ids):
    devices = blks * dirs
    cycles, turn = sky_map.shape[1:]
    orders = legendre.shape[0]
    vmem = pl.BlockSpec(memory_space=pltpu.VMEM)
    hbm = pl.BlockSpec(memory_space=pltpu.HBM)
    slots = jax.ShapeDtypeStruct((blks * orders, LANES), jnp.float32)
    sky_map, legendre, wigner, wavelet, order_ids, dir_ids = (pltpu.with_memory_space_constraint(x, pltpu.HBM) for x in (sky_map, legendre, wigner, wavelet, order_ids, dir_ids))
    mixed, columns = pl.pallas_call(
        functools.partial(spectra_kernel, blks, dirs),
        out_shape=(slots, jax.ShapeDtypeStruct(slots.shape, jnp.int32)),
        in_specs=[hbm] * 6,
        out_specs=(vmem, vmem),
        scratch_shapes=[
            pltpu.SMEM(order_ids.shape, jnp.int32),
            pltpu.SMEM(dir_ids.shape, jnp.int32),
            pltpu.VMEM(sky_map.shape, jnp.float32),
            pltpu.VMEM(legendre.shape, jnp.float32),
            pltpu.VMEM(wigner.shape, jnp.float32),
            pltpu.VMEM(wavelet.shape, jnp.float32),
            pltpu.VMEM((blks, 1, LANES), jnp.float32),
            pltpu.VMEM((devices, 1, LANES), jnp.float32),
            pltpu.VMEM((blks, orders, LANES), jnp.float32),
            pltpu.VMEM((devices, orders, LANES), jnp.float32),
            pltpu.SemaphoreType.DMA((6,)),
            pltpu.SemaphoreType.DMA((2,)),
            pltpu.SemaphoreType.DMA((2,)),
        ],
        compiler_params=pltpu.CompilerParams(
            collective_id=0, has_side_effects=True, vmem_limit_bytes=48 * 2**20
        ),
    )(order_ids, dir_ids, sky_map, legendre, wigner, wavelet)
    several = blks * orders > 32
    total_shape = (turn // INNER // 2, LANES, 2 * INNER) if several else (1, 8, LANES)
    return pl.pallas_call(
        functools.partial(maps_kernel, turn, dirs, cycles),
        out_shape=jax.ShapeDtypeStruct((1, dirs, cycles, turn), jnp.float32),
        in_specs=[vmem, vmem],
        out_specs=vmem,
        scratch_shapes=[pltpu.VMEM(total_shape, jnp.float32)],
        compiler_params=pltpu.CompilerParams(vmem_limit_bytes=48 * 2**20),
    )(columns, mixed)


def solution(mesh):
    return jax.shard_map(
        functools.partial(local, mesh.shape["blk"], mesh.shape["dir"]),
        mesh=mesh,
        in_specs=(
            P("dir", "blk", None),
            P(),
            P("blk", None, None),
            P("dir", "blk", None, None),
            P("dir", None),
            P(),
        ),
        out_specs=P("dir", None, "blk", None),
        check_vma=False,
    )
```

```python
import functools
import math

import jax
import jax.numpy as jnp
from jax import lax
from jax.experimental import pallas as pl
from jax.experimental.pallas import tpu as pltpu
from jax.sharding import PartitionSpec as P

L = 4096
INNER = 512
LANES = 128
MESH = pl.DeviceIdType.MESH


def sin_turn(phase, turn):
    quarter = turn // 4
    shifted = lax.bitwise_and(phase + quarter, turn - 1)
    folded = quarter - jnp.abs(shifted - 2 * quarter)
    u = folded.astype(jnp.float32) * (1.0 / quarter)
    square = u * u
    half = math.pi / 2
    total = jnp.full_like(u, -(half**11) / math.factorial(11))
    for power in (9, 7, 5, 3, 1):
        sign = 1.0 if power % 4 == 1 else -1.0
        total = total * square + sign * half**power / math.factorial(power)
    return total * u


def halves(value):
    high = value.astype(jnp.bfloat16)
    low = (value - high.astype(jnp.float32)).astype(jnp.bfloat16)
    return high, low


def iota(shape, dim):
    return lax.broadcasted_iota(jnp.int32, shape, dim)


def column_of(scalars, row, rows_of):
    value = jnp.full(row.shape, scalars[0], jnp.int32)
    for index in range(1, len(scalars)):
        value = jnp.where(rows_of(row) == index, scalars[index], value)
    return value


def dot(a, b, dims):
    return lax.dot_general(a, b, (dims, ((), ())), preferred_element_type=jnp.float32)


def spectra_kernel(
    blks, dirs, order_hbm, dir_hbm, sky_hbm, legendre_hbm, wigner_hbm, wavelet_hbm,
    mixed_ref, table_ref, turn_ref, order_ref, dir_ref, sky_ref, legendre_ref, wigner_ref, wavelet_ref,
    send1, recv1, send2, recv2, in_sem, send_sem, recv_sem,
):
    blk, own = lax.axis_index("blk"), lax.axis_index("dir")
    devices = blks * dirs
    own_slot = own * blks + blk
    cycles, turn = sky_ref.shape[1], sky_ref.shape[2]
    orders, degrees, thetas = legendre_ref.shape
    steps = turn // INNER
    groups = LANES // cycles
    maps = dirs

    barrier = pltpu.get_barrier_semaphore()

    power = devices & (devices - 1) == 0

    def partner(step):
        place = blk * dirs + own
        other = lax.bitwise_xor(place, devices - step) if power else lax.rem(place + step, devices)
        return lax.div(other, dirs), lax.rem(other, dirs)

    def for_partners(body):
        lax.fori_loop(1, devices, lambda step, carry: body(*partner(step)), None, unroll=1)

    def greet(other_blk, other_dir):
        pl.semaphore_signal(
            barrier, inc=1, device_id=(other_blk, other_dir), device_id_type=MESH)

    for_partners(greet)
    loads = [
        pltpu.make_async_copy(source, target, in_sem.at[index])
        for index, (source, target) in enumerate((
            (order_hbm, order_ref), (sky_hbm, sky_ref), (dir_hbm, dir_ref),
            (legendre_hbm, legendre_ref), (wigner_hbm, wigner_ref), (wavelet_hbm, wavelet_ref),
        ))
    ]
    for load in loads:
        load.start()

    loads[0].wait()
    loads[1].wait()
    pieces = [sky_ref[0, :, a * INNER:(a + 1) * INNER] for a in range(steps)]
    sky_high, sky_low = halves(jnp.concatenate(pieces, axis=0))
    sky_both = jnp.concatenate([sky_high, sky_low], axis=0)
    rows = 2 * orders
    width = steps * cycles
    tile_row = iota((rows, LANES), 0)
    lane = iota((rows, LANES), 1)
    scale = 1.0 / math.sqrt(turn)

    def spectrum(group, carry):
        ids = []
        for j in range(groups):
            base = (group * groups + j) * orders
            ids.append(column_of(
                [order_ref[base + s] for s in range(orders)], tile_row,
                lambda r: lax.rem(r, orders),
            ))
        column = jnp.concatenate(ids, axis=0)
        tall = groups * rows
        part = lax.rem(lax.div(iota((tall, LANES), 0), orders), 2)
        offset = (1 + part) * (turn // 4)
        position = iota((tall, LANES), 1)
        table = jnp.concatenate(
            [sin_turn(column * (position + LANES * c) + offset, turn) for c in range(INNER // LANES)],
            axis=1,
        )
        table_high, table_low = halves(table)
        product = dot(jnp.concatenate([table_high, table_low], axis=0), sky_both, ((1,), (1,)))
        inner = product[:tall, :width] + product[:tall, width:] + product[tall:, :width]
        swapped = jnp.concatenate(
            [
                piece
                for j in range(groups)
                for piece in (
                    inner[j * rows + orders:(j + 1) * rows], inner[j * rows:j * rows + orders])
            ],
            axis=0,
        )
        total = jnp.zeros((tall, LANES), jnp.float32)
        for c in range(width // LANES):
            phase = column * (lax.div(position + LANES * c, cycles) * INNER)
            cut = slice(c * LANES, (c + 1) * LANES)
            total += sin_turn(phase + turn // 4, turn) * inner[:, cut]
            total += sin_turn(phase + part * (turn // 2), turn) * swapped[:, cut]
        shift = LANES // 2
        while shift >= cycles:
            total = total + pltpu.roll(total, shift, 1)
            shift //= 2
        total = total * scale
        for j in range(groups):
            block = jnp.where(lax.div(lane, cycles) == tile_row, total[j * rows:(j + 1) * rows], 0.0)
            send1[group * groups + j] = jnp.sum(block, axis=0, keepdims=True)
        return carry

    lax.fori_loop(0, blks // groups, spectrum, 0, unroll=blks == groups)

    pl.semaphore_wait(barrier, devices - 1)

    def scatter(send, recv, phase):
        def one(other_blk, other_dir):
            pltpu.make_async_remote_copy(
                src_ref=send.at[other_blk], dst_ref=recv.at[own_slot],
                send_sem=send_sem.at[phase], recv_sem=recv_sem.at[phase],
                device_id=(other_blk, other_dir), device_id_type=MESH,
            ).start()

        for_partners(one)
        recv[own_slot] = send[blk]

    def settle(recv, sem, phase):
        span = recv.at[pl.ds(0, devices - 1)]
        pltpu.make_async_copy(span, span, sem.at[phase]).wait()

    scatter(send1, recv1, 0)

    for load in loads[2:]:
        load.wait()
    flat = orders * degrees
    legendre_both = jnp.concatenate(halves(legendre_ref[...].reshape(flat, thetas)), axis=0)
    wigner_high, wigner_low = halves(wigner_ref[0].reshape(flat, thetas))
    tall = maps * rows
    own_ids = column_of(
        [order_ref[blk * orders + s] for s in range(orders)], iota((tall, flat), 0),
        lambda r: lax.rem(r, orders),
    )
    place = iota((tall, flat), 1)
    same = lax.div(place, degrees) == lax.rem(iota((tall, flat), 0), orders)
    live = L - degrees + lax.rem(place, degrees) >= own_ids
    weight = jnp.concatenate([wavelet_ref[...]] * orders, axis=1)
    weight = jnp.where(same & live, weight, 0.0)

    settle(recv1, recv_sem, 0)

    spectra = []
    for p in range(maps):
        chunks = []
        for g in range(blks // groups):
            start = p * blks + g * groups
            block = recv1[start:start + groups].reshape(groups, LANES)
            out = jnp.where(lax.div(lane, cycles) == tile_row, block, 0.0)
            for shift in range(1, groups):
                turned = pltpu.roll(pltpu.roll(block, groups - shift, 0), shift * cycles, 1)
                hit = lax.div(lane, cycles) == lax.rem(tile_row + shift, groups)
                out = jnp.where(hit, turned, out)
            chunks.append(out)
        spectra.append(jnp.concatenate(chunks, axis=1))
    both = jnp.concatenate(halves(jnp.concatenate(spectra, axis=0)), axis=0)
    product = dot(both, legendre_both, ((1,), (1,)))
    coeffs = product[:tall, :flat] + product[:tall, flat:] + product[tall:, :flat]
    both = jnp.concatenate(halves(coeffs * weight), axis=0)
    first = dot(both, wigner_high, ((1,), (0,)))
    second = dot(both[:tall], wigner_low, ((1,), (0,)))
    component = first[:tall] + first[tall:] + second

    for h in range(thetas // LANES):
        turned = [
            [
                block if shift == 0 else pltpu.roll(block, shift * cycles, 1)
                for shift in range(groups)
            ]
            for block in (
                component[p * rows:(p + 1) * rows, h * LANES:(h + 1) * LANES] for p in range(maps)
            )
        ]
        for j in range(groups):
            block = turned[0][(-j) % groups]
            for target in range(1, groups):
                block = jnp.where(
                    lax.div(lane, cycles) == target,
                    turned[target % maps][(target - j) % groups], block,
                )
            send2[h * groups + j] = jnp.where(
                lane[:orders] < LANES // 2, block[:orders], block[orders:]
            )

    scatter(send2, recv2, 1)

    slab = groups * orders
    levels = (steps - 1).bit_length()

    def put_tables(chunk, carry):
        column = jnp.concatenate(
            [
                column_of(
                    [order_ref[chunk * slab + 8 * q + s] for s in range(8)], tile_row, lambda r: r)
                for q in range(slab // 8)
            ],
            axis=0,
        )
        place = iota((slab, LANES), 1)
        phases = [column * (place + LANES * c) for c in range(INNER // LANES)]
        cosine = jnp.concatenate([sin_turn(x + turn // 4, turn) for x in phases], axis=1)
        sine = jnp.concatenate([sin_turn(x, turn) for x in phases], axis=1)
        table = jnp.concatenate(
            [
                jnp.concatenate([cosine, sine], axis=1),
                jnp.concatenate([-sine, cosine], axis=1),
            ],
            axis=0,
        )
        table_high, table_low = halves(table)
        tall = 6 * slab
        table_ref[pl.ds(pl.multiple_of(chunk * tall, tall), tall), :] = jnp.concatenate(
            [table_high, table_high, table_low], axis=0)
        for level in range(levels):
            phase = column * (INNER << level)
            sine = sin_turn(phase, turn)
            turn_ref[chunk, 2 * level] = sin_turn(phase + turn // 4, turn)
            turn_ref[chunk, 2 * level + 1] = jnp.where(place < LANES // 2, -sine, sine)
        return carry

    lax.fori_loop(0, blks // groups, put_tables, 0, unroll=blks == groups)

    direction = dir_ref[own]
    half_lane = iota((blks * orders, LANES), 1) < LANES // 2

    factors = []
    for i in range(dirs):
        azimuth = 2 * i - dirs + 1
        phase = jnp.full((blks * orders, LANES), direction, jnp.int32)
        phase = phase * (azimuth * (turn // (2 * dirs))) + 4 * turn
        sine = sin_turn(phase, turn)
        factors.append((sin_turn(phase + turn // 4, turn), jnp.where(half_lane, sine, -sine)))

    settle(recv2, recv_sem, 1)

    mixed = jnp.zeros((blks * orders, LANES), jnp.float32)
    crossed = jnp.zeros((blks * orders, LANES), jnp.float32)
    for i, (along, across) in enumerate(factors):
        value = recv2[i * blks:(i + 1) * blks].reshape(blks * orders, LANES)
        mixed += along * value
        crossed += across * value
    mixed = mixed + pltpu.roll(crossed, LANES // 2, 1)
    mixed_ref[...] = mixed

    settle(recv1, send_sem, 0)
    settle(recv2, send_sem, 1)


def maps_kernel(turn, maps, cycles, mixed_ref, table_ref, turn_ref, out_hbm, out_ref, total, out_sem):
    slab = 32
    steps = turn // INNER
    chunks = mixed_ref.shape[0] // slab
    lane = iota((slab, LANES), 1)
    real = lane < LANES // 2
    writes = []

    def maps_of(chunk, last):
        tall = 6 * slab
        right = table_ref[pl.ds(pl.multiple_of(chunk * tall, tall), tall), :]
        turns = [mixed_ref[pl.ds(chunk * slab, slab), :]]
        while len(turns) < steps:
            level = 2 * (len(turns).bit_length() - 1)
            along, across = turn_ref[chunk, level], turn_ref[chunk, level + 1]
            turns = turns + [
                along * value + across * pltpu.roll(value, LANES // 2, 1) for value in turns
            ]
        for pair in range(steps // 2):
            one, two = turns[2 * pair], turns[2 * pair + 1]
            left = jnp.concatenate(
                [
                    jnp.where(real, one, pltpu.roll(two, LANES // 2, 1)),
                    jnp.where(real, pltpu.roll(one, LANES // 2, 1), two),
                ],
                axis=0,
            )
            left_high, left_low = halves(left)
            left = jnp.concatenate([left_high, left_low, left_high], axis=0)
            value = dot(left, right, ((0,), (0,)))
            if chunks > 1:
                value = value + total[pair]
                total[pair] = value
            if last:
                real_part, imag_part = value[:, :INNER], value[:, INNER:]
                power = real_part * real_part + imag_part * imag_part
                modulus = power * lax.rsqrt(jnp.maximum(power, 1e-37))
                half = maps * cycles
                for part in range(2):
                    a = 2 * pair + part
                    out_ref[0, :, :, a * INNER:(a + 1) * INNER] = modulus[
                        part * half:(part + 1) * half
                    ].reshape(maps, cycles, INNER)
                cut = pl.ds(2 * pair * INNER, 2 * INNER)
                write = pltpu.make_async_copy(
                    out_ref.at[:, :, :, cut], out_hbm.at[:, :, :, cut], out_sem.at[pair])
                write.start()
                writes.append(write)

    if chunks > 1:
        total[...] = jnp.zeros_like(total)

        def partial(chunk, carry):
            maps_of(chunk, False)
            return carry

        lax.fori_loop(0, chunks - 1, partial, 0)
    maps_of(chunks - 1, True)
    for write in writes:
        write.wait()


def local(blks, dirs, sky_map, order_ids, legendre, wigner, wavelet, dir_ids):
    devices = blks * dirs
    cycles, turn = sky_map.shape[1:]
    orders = legendre.shape[0]
    vmem = pl.BlockSpec(memory_space=pltpu.VMEM)
    hbm = pl.BlockSpec(memory_space=pltpu.HBM)
    slots = jax.ShapeDtypeStruct((blks * orders, LANES), jnp.float32)
    sky_map, legendre, wigner, wavelet, order_ids, dir_ids = (pltpu.with_memory_space_constraint(x, pltpu.HBM) for x in (sky_map, legendre, wigner, wavelet, order_ids, dir_ids))
    slab = LANES // cycles * orders
    chunks = blks * orders // slab
    table = jax.ShapeDtypeStruct((chunks * 6 * slab, 2 * INNER), jnp.bfloat16)
    levels = (turn // INNER - 1).bit_length()
    turns = jax.ShapeDtypeStruct((chunks, 2 * levels, slab, LANES), jnp.float32)
    middle = pl.pallas_call(
        functools.partial(spectra_kernel, blks, dirs),
        out_shape=(slots, table, turns),
        in_specs=[hbm] * 6,
        out_specs=(vmem, vmem, vmem),
        scratch_shapes=[
            pltpu.SMEM(order_ids.shape, jnp.int32),
            pltpu.SMEM(dir_ids.shape, jnp.int32),
            pltpu.VMEM(sky_map.shape, jnp.float32),
            pltpu.VMEM(legendre.shape, jnp.float32),
            pltpu.VMEM(wigner.shape, jnp.float32),
            pltpu.VMEM(wavelet.shape, jnp.float32),
            pltpu.VMEM((blks, 1, LANES), jnp.float32),
            pltpu.VMEM((devices, 1, LANES), jnp.float32),
            pltpu.VMEM((blks, orders, LANES), jnp.float32),
            pltpu.VMEM((devices, orders, LANES), jnp.float32),
            pltpu.SemaphoreType.DMA((6,)),
            pltpu.SemaphoreType.DMA((2,)),
            pltpu.SemaphoreType.DMA((2,)),
        ],
        compiler_params=pltpu.CompilerParams(
            collective_id=0, has_side_effects=True, vmem_limit_bytes=48 * 2**20
        ),
    )(order_ids, dir_ids, sky_map, legendre, wigner, wavelet)
    several = chunks > 1
    total_shape = (turn // INNER // 2, LANES, 2 * INNER) if several else (1, 8, LANES)
    out = jax.ShapeDtypeStruct((1, dirs, cycles, turn), jnp.float32)
    return pl.pallas_call(
        functools.partial(maps_kernel, turn, dirs, cycles),
        out_shape=out,
        in_specs=[vmem] * 3,
        out_specs=hbm,
        scratch_shapes=[
            pltpu.VMEM(out.shape, jnp.float32),
            pltpu.VMEM(total_shape, jnp.float32),
            pltpu.SemaphoreType.DMA((turn // INNER // 2,)),
        ],
        compiler_params=pltpu.CompilerParams(vmem_limit_bytes=48 * 2**20),
    )(*middle)


def solution(mesh):
    return jax.shard_map(
        functools.partial(local, mesh.shape["blk"], mesh.shape["dir"]),
        mesh=mesh,
        in_specs=(
            P("dir", "blk", None),
            P(),
            P("blk", None, None),
            P("dir", "blk", None, None),
            P("dir", None),
            P(),
        ),
        out_specs=P("dir", None, "blk", None),
        check_vma=False,
    )
```

```python
import functools
import math

import jax
import jax.numpy as jnp
from jax import lax
from jax.experimental import pallas as pl
from jax.experimental.pallas import tpu as pltpu
from jax.sharding import PartitionSpec as P

L = 4096
INNER = 512
LANES = 128
MESH = pl.DeviceIdType.MESH


def sin_turn(phase, turn):
    quarter = turn // 4
    shifted = lax.bitwise_and(phase + quarter, turn - 1)
    folded = quarter - jnp.abs(shifted - 2 * quarter)
    u = folded.astype(jnp.float32) * (1.0 / quarter)
    square = u * u
    half = math.pi / 2
    total = jnp.full_like(u, -(half**11) / math.factorial(11))
    for power in (9, 7, 5, 3, 1):
        sign = 1.0 if power % 4 == 1 else -1.0
        total = total * square + sign * half**power / math.factorial(power)
    return total * u


def halves(value):
    high = value.astype(jnp.bfloat16)
    low = (value - high.astype(jnp.float32)).astype(jnp.bfloat16)
    return high, low


def iota(shape, dim):
    return lax.broadcasted_iota(jnp.int32, shape, dim)


def column_of(scalars, row, rows_of):
    value = jnp.full(row.shape, scalars[0], jnp.int32)
    for index in range(1, len(scalars)):
        value = jnp.where(rows_of(row) == index, scalars[index], value)
    return value


def dot(a, b, dims):
    return lax.dot_general(a, b, (dims, ((), ())), preferred_element_type=jnp.float32)


def spectra_kernel(
    blks, dirs, order_hbm, dir_hbm, sky_hbm, legendre_hbm, wigner_hbm, wavelet_hbm,
    mixed_ref, table_ref, turn_ref, order_ref, dir_ref, sky_ref, legendre_ref, wigner_ref, wavelet_ref,
    send1, recv1, send2, recv2, in_sem, send_sem, recv_sem,
):
    blk, own = lax.axis_index("blk"), lax.axis_index("dir")
    devices = blks * dirs
    own_slot = own * blks + blk
    cycles, turn = sky_ref.shape[1], sky_ref.shape[2]
    orders, degrees, thetas = legendre_ref.shape
    steps = turn // INNER
    groups = LANES // cycles
    maps = dirs

    barrier = pltpu.get_barrier_semaphore()

    power = devices & (devices - 1) == 0

    def partner(step):
        place = blk * dirs + own
        other = lax.bitwise_xor(place, devices - step) if power else lax.rem(place + step, devices)
        return lax.div(other, dirs), lax.rem(other, dirs)

    def for_partners(body):
        lax.fori_loop(1, devices, lambda step, carry: body(*partner(step)), None, unroll=1)

    def greet(other_blk, other_dir):
        pl.semaphore_signal(
            barrier, inc=1, device_id=(other_blk, other_dir), device_id_type=MESH)

    for_partners(greet)
    loads = [
        pltpu.make_async_copy(source, target, in_sem.at[index])
        for index, (source, target) in enumerate((
            (order_hbm, order_ref), (sky_hbm, sky_ref), (dir_hbm, dir_ref),
            (legendre_hbm, legendre_ref), (wigner_hbm, wigner_ref), (wavelet_hbm, wavelet_ref),
        ))
    ]
    for load in loads:
        load.start()

    loads[0].wait()
    loads[1].wait()
    pieces = [sky_ref[0, :, a * INNER:(a + 1) * INNER] for a in range(steps)]
    sky_high, sky_low = halves(jnp.concatenate(pieces, axis=0))
    sky_both = jnp.concatenate([sky_high, sky_low], axis=0)
    rows = 2 * orders
    width = steps * cycles
    tile_row = iota((rows, LANES), 0)
    lane = iota((rows, LANES), 1)
    scale = 1.0 / math.sqrt(turn)

    def spectrum(group, carry):
        ids = []
        for j in range(groups):
            base = (group * groups + j) * orders
            ids.append(column_of(
                [order_ref[base + s] for s in range(orders)], tile_row,
                lambda r: lax.rem(r, orders),
            ))
        column = jnp.concatenate(ids, axis=0)
        tall = groups * rows
        part = lax.rem(lax.div(iota((tall, LANES), 0), orders), 2)
        offset = (1 + part) * (turn // 4)
        position = iota((tall, LANES), 1)
        table = jnp.concatenate(
            [sin_turn(column * (position + LANES * c) + offset, turn) for c in range(INNER // LANES)],
            axis=1,
        )
        table_high, table_low = halves(table)
        product = dot(jnp.concatenate([table_high, table_low], axis=0), sky_both, ((1,), (1,)))
        inner = product[:tall, :width] + product[:tall, width:] + product[tall:, :width]
        swapped = jnp.concatenate(
            [
                piece
                for j in range(groups)
                for piece in (
                    inner[j * rows + orders:(j + 1) * rows], inner[j * rows:j * rows + orders])
            ],
            axis=0,
        )
        total = jnp.zeros((tall, LANES), jnp.float32)
        for c in range(width // LANES):
            phase = column * (lax.div(position + LANES * c, cycles) * INNER)
            cut = slice(c * LANES, (c + 1) * LANES)
            total += sin_turn(phase + turn // 4, turn) * inner[:, cut]
            total += sin_turn(phase + part * (turn // 2), turn) * swapped[:, cut]
        shift = LANES // 2
        while shift >= cycles:
            total = total + pltpu.roll(total, shift, 1)
            shift //= 2
        total = total * scale
        for j in range(groups):
            block = jnp.where(lax.div(lane, cycles) == tile_row, total[j * rows:(j + 1) * rows], 0.0)
            send1[group * groups + j] = jnp.sum(block, axis=0, keepdims=True)
        return carry

    lax.fori_loop(0, blks // groups, spectrum, 0, unroll=blks == groups)

    pl.semaphore_wait(barrier, devices - 1)

    def scatter(send, recv, phase):
        def one(other_blk, other_dir):
            pltpu.make_async_remote_copy(
                src_ref=send.at[other_blk], dst_ref=recv.at[own_slot],
                send_sem=send_sem.at[phase], recv_sem=recv_sem.at[phase],
                device_id=(other_blk, other_dir), device_id_type=MESH,
            ).start()

        for_partners(one)
        recv[own_slot] = send[blk]

    def settle(recv, sem, phase):
        span = recv.at[pl.ds(0, devices - 1)]
        pltpu.make_async_copy(span, span, sem.at[phase]).wait()

    scatter(send1, recv1, 0)

    for load in loads[2:]:
        load.wait()
    flat = orders * degrees
    legendre_both = jnp.concatenate(halves(legendre_ref[...].reshape(flat, thetas)), axis=0)
    wigner_high, wigner_low = halves(wigner_ref[0].reshape(flat, thetas))
    tall = maps * rows
    own_ids = column_of(
        [order_ref[blk * orders + s] for s in range(orders)], iota((tall, flat), 0),
        lambda r: lax.rem(r, orders),
    )
    place = iota((tall, flat), 1)
    same = lax.div(place, degrees) == lax.rem(iota((tall, flat), 0), orders)
    live = L - degrees + lax.rem(place, degrees) >= own_ids
    weight = jnp.concatenate([wavelet_ref[...]] * orders, axis=1)
    weight = jnp.where(same & live, weight, 0.0)

    settle(recv1, recv_sem, 0)

    spectra = []
    for p in range(maps):
        chunks = []
        for g in range(blks // groups):
            start = p * blks + g * groups
            block = recv1[start:start + groups].reshape(groups, LANES)
            out = jnp.where(lax.div(lane, cycles) == tile_row, block, 0.0)
            for shift in range(1, groups):
                turned = pltpu.roll(pltpu.roll(block, groups - shift, 0), shift * cycles, 1)
                hit = lax.div(lane, cycles) == lax.rem(tile_row + shift, groups)
                out = jnp.where(hit, turned, out)
            chunks.append(out)
        spectra.append(jnp.concatenate(chunks, axis=1))
    both = jnp.concatenate(halves(jnp.concatenate(spectra, axis=0)), axis=0)
    product = dot(both, legendre_both, ((1,), (1,)))
    coeffs = product[:tall, :flat] + product[:tall, flat:] + product[tall:, :flat]
    both = jnp.concatenate(halves(coeffs * weight), axis=0)
    first = dot(both, wigner_high, ((1,), (0,)))
    second = dot(both[:tall], wigner_low, ((1,), (0,)))
    component = first[:tall] + first[tall:] + second

    for h in range(thetas // LANES):
        turned = [
            [
                block if shift == 0 else pltpu.roll(block, shift * cycles, 1)
                for shift in range(groups)
            ]
            for block in (
                component[p * rows:(p + 1) * rows, h * LANES:(h + 1) * LANES] for p in range(maps)
            )
        ]
        for j in range(groups):
            block = turned[0][(-j) % groups]
            for target in range(1, groups):
                block = jnp.where(
                    lax.div(lane, cycles) == target,
                    turned[target % maps][(target - j) % groups], block,
                )
            send2[h * groups + j] = jnp.where(
                lane[:orders] < LANES // 2, block[:orders], block[orders:]
            )

    scatter(send2, recv2, 1)

    slab = groups * orders

    def put_tables(chunk, carry):
        column = jnp.concatenate(
            [
                column_of(
                    [order_ref[chunk * slab + 8 * q + s] for s in range(8)], tile_row, lambda r: r)
                for q in range(slab // 8)
            ],
            axis=0,
        )
        place = iota((slab, LANES), 1)
        phases = [column * (place + LANES * c) for c in range(INNER // LANES)]
        cosine = jnp.concatenate([sin_turn(x + turn // 4, turn) for x in phases], axis=1)
        sine = jnp.concatenate([sin_turn(x, turn) for x in phases], axis=1)
        table = jnp.concatenate(
            [
                jnp.concatenate([cosine, sine], axis=1),
                jnp.concatenate([-sine, cosine], axis=1),
            ],
            axis=0,
        )
        table_high, table_low = halves(table)
        tall = 6 * slab
        table_ref[pl.ds(pl.multiple_of(chunk * tall, tall), tall), :] = jnp.concatenate(
            [table_high, table_high, table_low], axis=0)
        for pair in range(steps // 2):
            phase = column * (INNER * (2 * pair + lax.div(place, LANES // 2)))
            turn_ref[chunk, pair, 0] = sin_turn(phase + turn // 4, turn)
            turn_ref[chunk, pair, 1] = sin_turn(phase, turn)
        return carry

    lax.fori_loop(0, blks // groups, put_tables, 0, unroll=blks == groups)

    direction = dir_ref[own]
    half_lane = iota((blks * orders, LANES), 1) < LANES // 2

    factors = []
    for i in range(dirs):
        azimuth = 2 * i - dirs + 1
        phase = jnp.full((blks * orders, LANES), direction, jnp.int32)
        phase = phase * (azimuth * (turn // (2 * dirs))) + 4 * turn
        sine = sin_turn(phase, turn)
        factors.append((sin_turn(phase + turn // 4, turn), jnp.where(half_lane, sine, -sine)))

    settle(recv2, recv_sem, 1)

    mixed = jnp.zeros((blks * orders, LANES), jnp.float32)
    crossed = jnp.zeros((blks * orders, LANES), jnp.float32)
    for i, (along, across) in enumerate(factors):
        value = recv2[i * blks:(i + 1) * blks].reshape(blks * orders, LANES)
        mixed += along * value
        crossed += across * value
    mixed = mixed + pltpu.roll(crossed, LANES // 2, 1)
    rolled = pltpu.roll(mixed, LANES // 2, 1)
    mixed_ref[0] = jnp.where(half_lane, mixed, rolled)
    mixed_ref[1] = jnp.where(half_lane, rolled, mixed)

    settle(recv1, send_sem, 0)
    settle(recv2, send_sem, 1)


def maps_kernel(turn, maps, cycles, mixed_ref, table_ref, turn_ref, out_hbm, out_ref, total, out_sem):
    slab = 32
    steps = turn // INNER
    chunks = mixed_ref.shape[1] // slab
    writes = []

    def maps_of(chunk, last):
        tall = 6 * slab
        right = table_ref[pl.ds(pl.multiple_of(chunk * tall, tall), tall), :]
        rows = pl.ds(chunk * slab, slab)
        mixed_real, mixed_imag = mixed_ref[0, rows, :], mixed_ref[1, rows, :]
        for pair in range(steps // 2):
            cosine, sine = turn_ref[chunk, pair, 0], turn_ref[chunk, pair, 1]
            left = jnp.concatenate(
                [
                    mixed_real * cosine - mixed_imag * sine,
                    mixed_real * sine + mixed_imag * cosine,
                ],
                axis=0,
            )
            left_high, left_low = halves(left)
            left = jnp.concatenate([left_high, left_low, left_high], axis=0)
            value = dot(left, right, ((0,), (0,)))
            if chunks > 1:
                value = value + total[pair]
                total[pair] = value
            if last:
                real_part, imag_part = value[:, :INNER], value[:, INNER:]
                modulus = jnp.sqrt(real_part * real_part + imag_part * imag_part)
                half = maps * cycles
                for part in range(2):
                    a = 2 * pair + part
                    out_ref[0, :, :, a * INNER:(a + 1) * INNER] = modulus[
                        part * half:(part + 1) * half
                    ].reshape(maps, cycles, INNER)
                cut = pl.ds(2 * pair * INNER, 2 * INNER)
                write = pltpu.make_async_copy(
                    out_ref.at[:, :, :, cut], out_hbm.at[:, :, :, cut], out_sem.at[pair])
                write.start()
                writes.append(write)

    if chunks > 1:
        total[...] = jnp.zeros_like(total)

        def partial(chunk, carry):
            maps_of(chunk, False)
            return carry

        lax.fori_loop(0, chunks - 1, partial, 0)
    maps_of(chunks - 1, True)
    for write in writes:
        write.wait()


def local(blks, dirs, sky_map, order_ids, legendre, wigner, wavelet, dir_ids):
    devices = blks * dirs
    cycles, turn = sky_map.shape[1:]
    orders = legendre.shape[0]
    vmem = pl.BlockSpec(memory_space=pltpu.VMEM)
    hbm = pl.BlockSpec(memory_space=pltpu.HBM)
    slots = jax.ShapeDtypeStruct((2, blks * orders, LANES), jnp.float32)
    sky_map, legendre, wigner, wavelet, order_ids, dir_ids = (pltpu.with_memory_space_constraint(x, pltpu.HBM) for x in (sky_map, legendre, wigner, wavelet, order_ids, dir_ids))
    slab = LANES // cycles * orders
    chunks = blks * orders // slab
    table = jax.ShapeDtypeStruct((chunks * 6 * slab, 2 * INNER), jnp.bfloat16)
    turns = jax.ShapeDtypeStruct((chunks, turn // INNER // 2, 2, slab, LANES), jnp.float32)
    middle = pl.pallas_call(
        functools.partial(spectra_kernel, blks, dirs),
        out_shape=(slots, table, turns),
        in_specs=[hbm] * 6,
        out_specs=(vmem, vmem, vmem),
        scratch_shapes=[
            pltpu.SMEM(order_ids.shape, jnp.int32),
            pltpu.SMEM(dir_ids.shape, jnp.int32),
            pltpu.VMEM(sky_map.shape, jnp.float32),
            pltpu.VMEM(legendre.shape, jnp.float32),
            pltpu.VMEM(wigner.shape, jnp.float32),
            pltpu.VMEM(wavelet.shape, jnp.float32),
            pltpu.VMEM((blks, 1, LANES), jnp.float32),
            pltpu.VMEM((devices, 1, LANES), jnp.float32),
            pltpu.VMEM((blks, orders, LANES), jnp.float32),
            pltpu.VMEM((devices, orders, LANES), jnp.float32),
            pltpu.SemaphoreType.DMA((6,)),
            pltpu.SemaphoreType.DMA((2,)),
            pltpu.SemaphoreType.DMA((2,)),
        ],
        compiler_params=pltpu.CompilerParams(
            collective_id=0, has_side_effects=True, vmem_limit_bytes=48 * 2**20
        ),
    )(order_ids, dir_ids, sky_map, legendre, wigner, wavelet)
    several = chunks > 1
    total_shape = (turn // INNER // 2, LANES, 2 * INNER) if several else (1, 8, LANES)
    out = jax.ShapeDtypeStruct((1, dirs, cycles, turn), jnp.float32)
    return pl.pallas_call(
        functools.partial(maps_kernel, turn, dirs, cycles),
        out_shape=out,
        in_specs=[vmem] * 3,
        out_specs=hbm,
        scratch_shapes=[
            pltpu.VMEM(out.shape, jnp.float32),
            pltpu.VMEM(total_shape, jnp.float32),
            pltpu.SemaphoreType.DMA((turn // INNER // 2,)),
        ],
        compiler_params=pltpu.CompilerParams(vmem_limit_bytes=48 * 2**20),
    )(*middle)


def solution(mesh):
    return jax.shard_map(
        functools.partial(local, mesh.shape["blk"], mesh.shape["dir"]),
        mesh=mesh,
        in_specs=(
            P("dir", "blk", None),
            P(),
            P("blk", None, None),
            P("dir", "blk", None, None),
            P("dir", None),
            P(),
        ),
        out_specs=P("dir", None, "blk", None),
        check_vma=False,
    )
```

```python
import functools
import math

import jax
import jax.numpy as jnp
from jax import lax
from jax.experimental import pallas as pl
from jax.experimental.pallas import tpu as pltpu
from jax.sharding import PartitionSpec as P

L = 4096
INNER = 512
LANES = 128
MESH = pl.DeviceIdType.MESH


def sin_turn(phase, turn):
    quarter = turn // 4
    shifted = lax.bitwise_and(phase + quarter, turn - 1)
    folded = quarter - jnp.abs(shifted - 2 * quarter)
    u = folded.astype(jnp.float32) * (1.0 / quarter)
    square = u * u
    half = math.pi / 2
    total = jnp.full_like(u, -(half**11) / math.factorial(11))
    for power in (9, 7, 5, 3, 1):
        sign = 1.0 if power % 4 == 1 else -1.0
        total = total * square + sign * half**power / math.factorial(power)
    return total * u


def halves(value):
    high = value.astype(jnp.bfloat16)
    low = (value - high.astype(jnp.float32)).astype(jnp.bfloat16)
    return high, low


def iota(shape, dim):
    return lax.broadcasted_iota(jnp.int32, shape, dim)


def column_of(scalars, row, rows_of):
    value = jnp.full(row.shape, scalars[0], jnp.int32)
    for index in range(1, len(scalars)):
        value = jnp.where(rows_of(row) == index, scalars[index], value)
    return value


def dot(a, b, dims):
    return lax.dot_general(a, b, (dims, ((), ())), preferred_element_type=jnp.float32)


def spectra_kernel(
    blks, dirs, order_hbm, dir_hbm, sky_hbm, legendre_hbm, wigner_hbm, wavelet_hbm,
    mixed_ref, table_ref, turn_ref, order_ref, dir_ref, sky_ref, legendre_ref, wigner_ref, wavelet_ref,
    send1, recv1, send2, recv2, in_sem, send_sem, recv_sem,
):
    blk, own = lax.axis_index("blk"), lax.axis_index("dir")
    devices = blks * dirs
    own_slot = own * blks + blk
    cycles, turn = sky_ref.shape[1], sky_ref.shape[2]
    orders, degrees, thetas = legendre_ref.shape
    steps = turn // INNER
    groups = LANES // cycles
    maps = dirs

    barrier = pltpu.get_barrier_semaphore()

    power = devices & (devices - 1) == 0

    def partner(step):
        place = blk * dirs + own
        other = lax.bitwise_xor(place, devices - step) if power else lax.rem(place + step, devices)
        return lax.div(other, dirs), lax.rem(other, dirs)

    def for_partners(body):
        lax.fori_loop(1, devices, lambda step, carry: body(*partner(step)), None, unroll=devices <= 32)

    def greet(other_blk, other_dir):
        pl.semaphore_signal(
            barrier, inc=1, device_id=(other_blk, other_dir), device_id_type=MESH)

    for_partners(greet)
    loads = [
        pltpu.make_async_copy(source, target, in_sem.at[index])
        for index, (source, target) in enumerate((
            (order_hbm, order_ref), (sky_hbm, sky_ref), (dir_hbm, dir_ref),
            (legendre_hbm, legendre_ref), (wigner_hbm, wigner_ref), (wavelet_hbm, wavelet_ref),
        ))
    ]
    for load in loads:
        load.start()

    loads[0].wait()
    loads[1].wait()
    pieces = [sky_ref[0, :, a * INNER:(a + 1) * INNER] for a in range(steps)]
    sky_high, sky_low = halves(jnp.concatenate(pieces, axis=0))
    sky_both = jnp.concatenate([sky_high, sky_low], axis=0)
    rows = 2 * orders
    width = steps * cycles
    tile_row = iota((rows, LANES), 0)
    lane = iota((rows, LANES), 1)
    scale = 1.0 / math.sqrt(turn)

    def spectrum(group, carry):
        ids = []
        for j in range(groups):
            base = (group * groups + j) * orders
            ids.append(column_of(
                [order_ref[base + s] for s in range(orders)], tile_row,
                lambda r: lax.rem(r, orders),
            ))
        column = jnp.concatenate(ids, axis=0)
        tall = groups * rows
        part = lax.rem(lax.div(iota((tall, LANES), 0), orders), 2)
        offset = (1 + part) * (turn // 4)
        position = iota((tall, LANES), 1)
        table = jnp.concatenate(
            [sin_turn(column * (position + LANES * c) + offset, turn) for c in range(INNER // LANES)],
            axis=1,
        )
        table_high, table_low = halves(table)
        product = dot(jnp.concatenate([table_high, table_low], axis=0), sky_both, ((1,), (1,)))
        inner = product[:tall, :width] + product[:tall, width:] + product[tall:, :width]
        swapped = jnp.concatenate(
            [
                piece
                for j in range(groups)
                for piece in (
                    inner[j * rows + orders:(j + 1) * rows], inner[j * rows:j * rows + orders])
            ],
            axis=0,
        )
        total = jnp.zeros((tall, LANES), jnp.float32)
        for c in range(width // LANES):
            phase = column * (lax.div(position + LANES * c, cycles) * INNER)
            cut = slice(c * LANES, (c + 1) * LANES)
            total += sin_turn(phase + turn // 4, turn) * inner[:, cut]
            total += sin_turn(phase + part * (turn // 2), turn) * swapped[:, cut]
        shift = LANES // 2
        while shift >= cycles:
            total = total + pltpu.roll(total, shift, 1)
            shift //= 2
        total = total * scale
        for j in range(groups):
            block = jnp.where(lax.div(lane, cycles) == tile_row, total[j * rows:(j + 1) * rows], 0.0)
            send1[group * groups + j] = jnp.sum(block, axis=0, keepdims=True)
        return carry

    lax.fori_loop(0, blks // groups, spectrum, 0, unroll=blks == groups)

    pl.semaphore_wait(barrier, devices - 1)

    def scatter(send, recv, phase):
        def one(other_blk, other_dir):
            pltpu.make_async_remote_copy(
                src_ref=send.at[other_blk], dst_ref=recv.at[own_slot],
                send_sem=send_sem.at[phase], recv_sem=recv_sem.at[phase],
                device_id=(other_blk, other_dir), device_id_type=MESH,
            ).start()

        for_partners(one)
        recv[own_slot] = send[blk]

    def settle(recv, sem, phase):
        span = recv.at[pl.ds(0, devices - 1)]
        pltpu.make_async_copy(span, span, sem.at[phase]).wait()

    scatter(send1, recv1, 0)

    for load in loads[2:]:
        load.wait()
    flat = orders * degrees
    legendre_both = jnp.concatenate(halves(legendre_ref[...].reshape(flat, thetas)), axis=0)
    wigner_high, wigner_low = halves(wigner_ref[0].reshape(flat, thetas))
    tall = maps * rows
    own_ids = column_of(
        [order_ref[blk * orders + s] for s in range(orders)], iota((tall, flat), 0),
        lambda r: lax.rem(r, orders),
    )
    place = iota((tall, flat), 1)
    same = lax.div(place, degrees) == lax.rem(iota((tall, flat), 0), orders)
    live = L - degrees + lax.rem(place, degrees) >= own_ids
    weight = jnp.concatenate([wavelet_ref[...]] * orders, axis=1)
    weight = jnp.where(same & live, weight, 0.0)

    settle(recv1, recv_sem, 0)

    spectra = []
    for p in range(maps):
        chunks = []
        for g in range(blks // groups):
            start = p * blks + g * groups
            block = recv1[start:start + groups].reshape(groups, LANES)
            out = jnp.where(lax.div(lane, cycles) == tile_row, block, 0.0)
            for shift in range(1, groups):
                turned = pltpu.roll(pltpu.roll(block, groups - shift, 0), shift * cycles, 1)
                hit = lax.div(lane, cycles) == lax.rem(tile_row + shift, groups)
                out = jnp.where(hit, turned, out)
            chunks.append(out)
        spectra.append(jnp.concatenate(chunks, axis=1))
    both = jnp.concatenate(halves(jnp.concatenate(spectra, axis=0)), axis=0)
    product = dot(both, legendre_both, ((1,), (1,)))
    coeffs = product[:tall, :flat] + product[:tall, flat:] + product[tall:, :flat]
    both = jnp.concatenate(halves(coeffs * weight), axis=0)
    first = dot(both, wigner_high, ((1,), (0,)))
    second = dot(both[:tall], wigner_low, ((1,), (0,)))
    component = first[:tall] + first[tall:] + second

    for h in range(thetas // LANES):
        turned = [
            [
                block if shift == 0 else pltpu.roll(block, shift * cycles, 1)
                for shift in range(groups)
            ]
            for block in (
                component[p * rows:(p + 1) * rows, h * LANES:(h + 1) * LANES] for p in range(maps)
            )
        ]
        for j in range(groups):
            block = turned[0][(-j) % groups]
            for target in range(1, groups):
                block = jnp.where(
                    lax.div(lane, cycles) == target,
                    turned[target % maps][(target - j) % groups], block,
                )
            send2[h * groups + j] = jnp.where(
                lane[:orders] < LANES // 2, block[:orders], block[orders:]
            )

    scatter(send2, recv2, 1)

    slab = groups * orders

    def put_tables(chunk, carry):
        column = jnp.concatenate(
            [
                column_of(
                    [order_ref[chunk * slab + 8 * q + s] for s in range(8)], tile_row, lambda r: r)
                for q in range(slab // 8)
            ],
            axis=0,
        )
        place = iota((slab, LANES), 1)
        phases = [column * (place + LANES * c) for c in range(INNER // LANES)]
        cosine = jnp.concatenate([sin_turn(x + turn // 4, turn) for x in phases], axis=1)
        sine = jnp.concatenate([sin_turn(x, turn) for x in phases], axis=1)
        table = jnp.concatenate(
            [
                jnp.concatenate([cosine, sine], axis=1),
                jnp.concatenate([-sine, cosine], axis=1),
            ],
            axis=0,
        )
        table_high, table_low = halves(table)
        tall = 6 * slab
        table_ref[pl.ds(pl.multiple_of(chunk * tall, tall), tall), :] = jnp.concatenate(
            [table_high, table_high, table_low], axis=0)
        for pair in range(steps // 2):
            phase = column * (INNER * (2 * pair + lax.div(place, LANES // 2)))
            turn_ref[chunk, pair, 0] = sin_turn(phase + turn // 4, turn)
            turn_ref[chunk, pair, 1] = sin_turn(phase, turn)
        return carry

    lax.fori_loop(0, blks // groups, put_tables, 0, unroll=blks == groups)

    direction = dir_ref[own]
    half_lane = iota((blks * orders, LANES), 1) < LANES // 2

    factors = []
    for i in range(dirs):
        azimuth = 2 * i - dirs + 1
        phase = jnp.full((blks * orders, LANES), direction, jnp.int32)
        phase = phase * (azimuth * (turn // (2 * dirs))) + 4 * turn
        sine = sin_turn(phase, turn)
        factors.append((sin_turn(phase + turn // 4, turn), jnp.where(half_lane, sine, -sine)))

    settle(recv1, send_sem, 0)
    settle(recv2, recv_sem, 1)

    mixed = jnp.zeros((blks * orders, LANES), jnp.float32)
    crossed = jnp.zeros((blks * orders, LANES), jnp.float32)
    for i, (along, across) in enumerate(factors):
        value = recv2[i * blks:(i + 1) * blks].reshape(blks * orders, LANES)
        mixed += along * value
        crossed += across * value
    mixed = mixed + pltpu.roll(crossed, LANES // 2, 1)
    rolled = pltpu.roll(mixed, LANES // 2, 1)
    mixed_ref[0] = jnp.where(half_lane, mixed, rolled)
    mixed_ref[1] = jnp.where(half_lane, rolled, mixed)

    settle(recv2, send_sem, 1)


def maps_kernel(turn, maps, cycles, mixed_ref, table_ref, turn_ref, out_hbm, out_ref, total, out_sem):
    slab = 32
    steps = turn // INNER
    chunks = mixed_ref.shape[1] // slab
    writes = []

    def maps_of(chunk, last):
        tall = 6 * slab
        right = table_ref[pl.ds(pl.multiple_of(chunk * tall, tall), tall), :]
        rows = pl.ds(chunk * slab, slab)
        mixed_real, mixed_imag = mixed_ref[0, rows, :], mixed_ref[1, rows, :]
        for pair in range(steps // 2):
            cosine, sine = turn_ref[chunk, pair, 0], turn_ref[chunk, pair, 1]
            left = jnp.concatenate(
                [
                    mixed_real * cosine - mixed_imag * sine,
                    mixed_real * sine + mixed_imag * cosine,
                ],
                axis=0,
            )
            left_high, left_low = halves(left)
            left = jnp.concatenate([left_high, left_low, left_high], axis=0)
            value = dot(left, right, ((0,), (0,)))
            if chunks > 1:
                value = value + total[pair]
                total[pair] = value
            if last:
                real_part, imag_part = value[:, :INNER], value[:, INNER:]
                modulus = jnp.sqrt(real_part * real_part + imag_part * imag_part)
                half = maps * cycles
                for part in range(2):
                    a = 2 * pair + part
                    out_ref[0, :, :, a * INNER:(a + 1) * INNER] = modulus[
                        part * half:(part + 1) * half
                    ].reshape(maps, cycles, INNER)
                cut = pl.ds(2 * pair * INNER, 2 * INNER)
                write = pltpu.make_async_copy(
                    out_ref.at[:, :, :, cut], out_hbm.at[:, :, :, cut], out_sem.at[pair])
                write.start()
                writes.append(write)

    if chunks > 1:
        total[...] = jnp.zeros_like(total)

        def partial(chunk, carry):
            maps_of(chunk, False)
            return carry

        lax.fori_loop(0, chunks - 1, partial, 0)
    maps_of(chunks - 1, True)
    for write in writes:
        write.wait()


def local(blks, dirs, sky_map, order_ids, legendre, wigner, wavelet, dir_ids):
    devices = blks * dirs
    cycles, turn = sky_map.shape[1:]
    orders = legendre.shape[0]
    vmem = pl.BlockSpec(memory_space=pltpu.VMEM)
    hbm = pl.BlockSpec(memory_space=pltpu.HBM)
    slots = jax.ShapeDtypeStruct((2, blks * orders, LANES), jnp.float32)
    sky_map, legendre, wigner, wavelet, order_ids, dir_ids = (pltpu.with_memory_space_constraint(x, pltpu.HBM) for x in (sky_map, legendre, wigner, wavelet, order_ids, dir_ids))
    slab = LANES // cycles * orders
    chunks = blks * orders // slab
    table = jax.ShapeDtypeStruct((chunks * 6 * slab, 2 * INNER), jnp.bfloat16)
    turns = jax.ShapeDtypeStruct((chunks, turn // INNER // 2, 2, slab, LANES), jnp.float32)
    middle = pl.pallas_call(
        functools.partial(spectra_kernel, blks, dirs),
        out_shape=(slots, table, turns),
        in_specs=[hbm] * 6,
        out_specs=(vmem, vmem, vmem),
        scratch_shapes=[
            pltpu.SMEM(order_ids.shape, jnp.int32),
            pltpu.SMEM(dir_ids.shape, jnp.int32),
            pltpu.VMEM(sky_map.shape, jnp.float32),
            pltpu.VMEM(legendre.shape, jnp.float32),
            pltpu.VMEM(wigner.shape, jnp.float32),
            pltpu.VMEM(wavelet.shape, jnp.float32),
            pltpu.VMEM((blks, 1, LANES), jnp.float32),
            pltpu.VMEM((devices, 1, LANES), jnp.float32),
            pltpu.VMEM((blks, orders, LANES), jnp.float32),
            pltpu.VMEM((devices, orders, LANES), jnp.float32),
            pltpu.SemaphoreType.DMA((6,)),
            pltpu.SemaphoreType.DMA((2,)),
            pltpu.SemaphoreType.DMA((2,)),
        ],
        compiler_params=pltpu.CompilerParams(
            collective_id=0, has_side_effects=True, vmem_limit_bytes=48 * 2**20
        ),
    )(order_ids, dir_ids, sky_map, legendre, wigner, wavelet)
    several = chunks > 1
    total_shape = (turn // INNER // 2, LANES, 2 * INNER) if several else (1, 8, LANES)
    out = jax.ShapeDtypeStruct((1, dirs, cycles, turn), jnp.float32)
    return pl.pallas_call(
        functools.partial(maps_kernel, turn, dirs, cycles),
        out_shape=out,
        in_specs=[vmem] * 3,
        out_specs=hbm,
        scratch_shapes=[
            pltpu.VMEM(out.shape, jnp.float32),
            pltpu.VMEM(total_shape, jnp.float32),
            pltpu.SemaphoreType.DMA((turn // INNER // 2,)),
        ],
        compiler_params=pltpu.CompilerParams(vmem_limit_bytes=48 * 2**20),
    )(*middle)


def solution(mesh):
    return jax.shard_map(
        functools.partial(local, mesh.shape["blk"], mesh.shape["dir"]),
        mesh=mesh,
        in_specs=(
            P("dir", "blk", None),
            P(),
            P("blk", None, None),
            P("dir", "blk", None, None),
            P("dir", None),
            P(),
        ),
        out_specs=P("dir", None, "blk", None),
        check_vma=False,
    )
```

```python
import functools
import math

import jax
import jax.numpy as jnp
from jax import lax
from jax.experimental import pallas as pl
from jax.experimental.pallas import tpu as pltpu
from jax.sharding import PartitionSpec as P

L = 4096
INNER = 512
LANES = 128
MESH = pl.DeviceIdType.MESH


def sin_turn(phase, turn):
    quarter = turn // 4
    shifted = lax.bitwise_and(phase + quarter, turn - 1)
    folded = quarter - jnp.abs(shifted - 2 * quarter)
    u = folded.astype(jnp.float32) * (1.0 / quarter)
    square = u * u
    half = math.pi / 2
    total = jnp.full_like(u, -(half**11) / math.factorial(11))
    for power in (9, 7, 5, 3, 1):
        sign = 1.0 if power % 4 == 1 else -1.0
        total = total * square + sign * half**power / math.factorial(power)
    return total * u


def halves(value):
    high = value.astype(jnp.bfloat16)
    low = (value - high.astype(jnp.float32)).astype(jnp.bfloat16)
    return high, low


def iota(shape, dim):
    return lax.broadcasted_iota(jnp.int32, shape, dim)


def column_of(scalars, row, rows_of):
    value = jnp.full(row.shape, scalars[0], jnp.int32)
    for index in range(1, len(scalars)):
        value = jnp.where(rows_of(row) == index, scalars[index], value)
    return value


def dot(a, b, dims):
    return lax.dot_general(a, b, (dims, ((), ())), preferred_element_type=jnp.float32)


def spectra_kernel(
    blks, dirs, order_hbm, dir_hbm, sky_hbm, legendre_hbm, wigner_hbm, wavelet_hbm,
    mixed_ref, table_ref, turn_ref, order_ref, dir_ref, sky_ref, legendre_ref, wigner_ref, wavelet_ref,
    send1, recv1, send2, recv2, in_sem, send_sem, recv_sem,
):
    blk, own = lax.axis_index("blk"), lax.axis_index("dir")
    devices = blks * dirs
    own_slot = own * blks + blk
    cycles, turn = sky_ref.shape[1], sky_ref.shape[2]
    orders, degrees, thetas = legendre_ref.shape
    steps = turn // INNER
    groups = LANES // cycles
    maps = dirs

    barrier = pltpu.get_barrier_semaphore()

    power = devices & (devices - 1) == 0

    def partner(step):
        place = blk * dirs + own
        other = lax.bitwise_xor(place, devices - step) if power else lax.rem(place + step, devices)
        return lax.div(other, dirs), lax.rem(other, dirs)

    def for_partners(body):
        lax.fori_loop(1, devices, lambda step, carry: body(*partner(step)), None, unroll=1)

    def greet(other_blk, other_dir):
        pl.semaphore_signal(
            barrier, inc=1, device_id=(other_blk, other_dir), device_id_type=MESH)

    for_partners(greet)
    loads = [
        pltpu.make_async_copy(source, target, in_sem.at[index])
        for index, (source, target) in enumerate((
            (order_hbm, order_ref), (sky_hbm, sky_ref), (dir_hbm, dir_ref),
            (legendre_hbm, legendre_ref), (wigner_hbm, wigner_ref), (wavelet_hbm, wavelet_ref),
        ))
    ]
    for load in loads:
        load.start()

    loads[0].wait()
    loads[1].wait()
    pieces = [sky_ref[0, :, a * INNER:(a + 1) * INNER] for a in range(steps)]
    sky_high, sky_low = halves(jnp.concatenate(pieces, axis=0))
    sky_both = jnp.concatenate([sky_high, sky_low], axis=0)
    rows = 2 * orders
    width = steps * cycles
    tile_row = iota((rows, LANES), 0)
    lane = iota((rows, LANES), 1)
    scale = 1.0 / math.sqrt(turn)

    def spectrum(group, carry):
        ids = []
        for j in range(groups):
            base = (group * groups + j) * orders
            ids.append(column_of(
                [order_ref[base + s] for s in range(orders)], tile_row,
                lambda r: lax.rem(r, orders),
            ))
        column = jnp.concatenate(ids, axis=0)
        tall = groups * rows
        part = lax.rem(lax.div(iota((tall, LANES), 0), orders), 2)
        offset = (1 + part) * (turn // 4)
        position = iota((tall, LANES), 1)
        table = jnp.concatenate(
            [sin_turn(column * (position + LANES * c) + offset, turn) for c in range(INNER // LANES)],
            axis=1,
        )
        table_high, table_low = halves(table)
        product = dot(jnp.concatenate([table_high, table_low], axis=0), sky_both, ((1,), (1,)))
        inner = product[:tall, :width] + product[:tall, width:] + product[tall:, :width]
        swapped = jnp.concatenate(
            [
                piece
                for j in range(groups)
                for piece in (
                    inner[j * rows + orders:(j + 1) * rows], inner[j * rows:j * rows + orders])
            ],
            axis=0,
        )
        total = jnp.zeros((tall, LANES), jnp.float32)
        for c in range(width // LANES):
            phase = column * (lax.div(position + LANES * c, cycles) * INNER)
            cut = slice(c * LANES, (c + 1) * LANES)
            total += sin_turn(phase + turn // 4, turn) * inner[:, cut]
            total += sin_turn(phase + part * (turn // 2), turn) * swapped[:, cut]
        shift = LANES // 2
        while shift >= cycles:
            total = total + pltpu.roll(total, shift, 1)
            shift //= 2
        total = total * scale
        for j in range(groups):
            block = jnp.where(lax.div(lane, cycles) == tile_row, total[j * rows:(j + 1) * rows], 0.0)
            send1[group * groups + j] = jnp.sum(block, axis=0, keepdims=True)
        return carry

    lax.fori_loop(0, blks // groups, spectrum, 0, unroll=blks == groups)

    pl.semaphore_wait(barrier, devices - 1)

    def scatter(send, recv, phase):
        def one(other_blk, other_dir):
            pltpu.make_async_remote_copy(
                src_ref=send.at[other_blk], dst_ref=recv.at[own_slot],
                send_sem=send_sem.at[phase], recv_sem=recv_sem.at[phase],
                device_id=(other_blk, other_dir), device_id_type=MESH,
            ).start()

        for_partners(one)
        recv[own_slot] = send[blk]

    def settle(recv, sem, phase):
        span = recv.at[pl.ds(0, devices - 1)]
        pltpu.make_async_copy(span, span, sem.at[phase]).wait()

    scatter(send1, recv1, 0)

    for load in loads[2:]:
        load.wait()
    flat = orders * degrees
    legendre_high, legendre_low = halves(legendre_ref[...].reshape(flat, thetas))
    legendre_both = jnp.concatenate([legendre_high, legendre_high, legendre_low], axis=1)
    wigner_high, wigner_low = halves(wigner_ref[0].reshape(flat, thetas))
    wigner_both = jnp.concatenate([wigner_high, wigner_high, wigner_low], axis=0)
    tall = maps * rows
    own_ids = column_of(
        [order_ref[blk * orders + s] for s in range(orders)], iota((tall, flat), 0),
        lambda r: lax.rem(r, orders),
    )
    place = iota((tall, flat), 1)
    same = lax.div(place, degrees) == lax.rem(iota((tall, flat), 0), orders)
    live = L - degrees + lax.rem(place, degrees) >= own_ids
    weight = jnp.concatenate([wavelet_ref[...]] * orders, axis=1)
    weight = jnp.where(same & live, weight, 0.0)

    settle(recv1, recv_sem, 0)

    spectra = []
    for p in range(maps):
        chunks = []
        for g in range(blks // groups):
            start = p * blks + g * groups
            block = recv1[start:start + groups].reshape(groups, LANES)
            out = jnp.where(lax.div(lane, cycles) == tile_row, block, 0.0)
            for shift in range(1, groups):
                turned = pltpu.roll(pltpu.roll(block, groups - shift, 0), shift * cycles, 1)
                hit = lax.div(lane, cycles) == lax.rem(tile_row + shift, groups)
                out = jnp.where(hit, turned, out)
            chunks.append(out)
        spectra.append(jnp.concatenate(chunks, axis=1))
    high, low = halves(jnp.concatenate(spectra, axis=0))
    coeffs = dot(jnp.concatenate([high, low, high], axis=1), legendre_both, ((1,), (1,)))
    high, low = halves(coeffs * weight)
    component = dot(jnp.concatenate([high, low, high], axis=1), wigner_both, ((1,), (0,)))

    for h in range(thetas // LANES):
        turned = [
            [
                block if shift == 0 else pltpu.roll(block, shift * cycles, 1)
                for shift in range(groups)
            ]
            for block in (
                component[p * rows:(p + 1) * rows, h * LANES:(h + 1) * LANES] for p in range(maps)
            )
        ]
        for j in range(groups):
            block = turned[0][(-j) % groups]
            for target in range(1, groups):
                block = jnp.where(
                    lax.div(lane, cycles) == target,
                    turned[target % maps][(target - j) % groups], block,
                )
            send2[h * groups + j] = jnp.where(
                lane[:orders] < LANES // 2, block[:orders], block[orders:]
            )

    scatter(send2, recv2, 1)

    slab = groups * orders

    def put_tables(chunk, carry):
        column = jnp.concatenate(
            [
                column_of(
                    [order_ref[chunk * slab + 8 * q + s] for s in range(8)], tile_row, lambda r: r)
                for q in range(slab // 8)
            ],
            axis=0,
        )
        place = iota((slab, LANES), 1)
        phases = [column * (place + LANES * c) for c in range(INNER // LANES)]
        cosine = jnp.concatenate([sin_turn(x + turn // 4, turn) for x in phases], axis=1)
        sine = jnp.concatenate([sin_turn(x, turn) for x in phases], axis=1)
        table = jnp.concatenate(
            [
                jnp.concatenate([cosine, sine], axis=1),
                jnp.concatenate([-sine, cosine], axis=1),
            ],
            axis=0,
        )
        table_high, table_low = halves(table)
        tall = 6 * slab
        table_ref[pl.ds(pl.multiple_of(chunk * tall, tall), tall), :] = jnp.concatenate(
            [table_high, table_high, table_low], axis=0)
        for pair in range(steps // 2):
            phase = column * (INNER * (2 * pair + lax.div(place, LANES // 2)))
            turn_ref[chunk, pair, 0] = sin_turn(phase + turn // 4, turn)
            turn_ref[chunk, pair, 1] = sin_turn(phase, turn)
        return carry

    lax.fori_loop(0, blks // groups, put_tables, 0, unroll=blks == groups)

    direction = dir_ref[own]
    half_lane = iota((blks * orders, LANES), 1) < LANES // 2

    factors = []
    for i in range(dirs):
        azimuth = 2 * i - dirs + 1
        phase = jnp.full((blks * orders, LANES), direction, jnp.int32)
        phase = phase * (azimuth * (turn // (2 * dirs))) + 4 * turn
        sine = sin_turn(phase, turn)
        factors.append((sin_turn(phase + turn // 4, turn), jnp.where(half_lane, sine, -sine)))

    settle(recv2, recv_sem, 1)

    mixed = jnp.zeros((blks * orders, LANES), jnp.float32)
    crossed = jnp.zeros((blks * orders, LANES), jnp.float32)
    for i, (along, across) in enumerate(factors):
        value = recv2[i * blks:(i + 1) * blks].reshape(blks * orders, LANES)
        mixed += along * value
        crossed += across * value
    mixed = mixed + pltpu.roll(crossed, LANES // 2, 1)
    rolled = pltpu.roll(mixed, LANES // 2, 1)
    mixed_ref[0] = jnp.where(half_lane, mixed, rolled)
    mixed_ref[1] = jnp.where(half_lane, rolled, mixed)

    settle(recv1, send_sem, 0)
    settle(recv2, send_sem, 1)


def maps_kernel(turn, maps, cycles, mixed_ref, table_ref, turn_ref, out_hbm, out_ref, total, out_sem):
    slab = 32
    steps = turn // INNER
    chunks = mixed_ref.shape[1] // slab
    writes = []

    def maps_of(chunk, last):
        tall = 6 * slab
        right = table_ref[pl.ds(pl.multiple_of(chunk * tall, tall), tall), :]
        rows = pl.ds(chunk * slab, slab)
        mixed_real, mixed_imag = mixed_ref[0, rows, :], mixed_ref[1, rows, :]
        for pair in range(steps // 2):
            cosine, sine = turn_ref[chunk, pair, 0], turn_ref[chunk, pair, 1]
            left = jnp.concatenate(
                [
                    mixed_real * cosine - mixed_imag * sine,
                    mixed_real * sine + mixed_imag * cosine,
                ],
                axis=0,
            )
            left_high, left_low = halves(left)
            left = jnp.concatenate([left_high, left_low, left_high], axis=0)
            value = dot(left, right, ((0,), (0,)))
            if chunks > 1:
                value = value + total[pair]
                total[pair] = value
            if last:
                real_part, imag_part = value[:, :INNER], value[:, INNER:]
                modulus = jnp.sqrt(real_part * real_part + imag_part * imag_part)
                half = maps * cycles
                for part in range(2):
                    a = 2 * pair + part
                    out_ref[0, :, :, a * INNER:(a + 1) * INNER] = modulus[
                        part * half:(part + 1) * half
                    ].reshape(maps, cycles, INNER)
                cut = pl.ds(2 * pair * INNER, 2 * INNER)
                write = pltpu.make_async_copy(
                    out_ref.at[:, :, :, cut], out_hbm.at[:, :, :, cut], out_sem.at[pair])
                write.start()
                writes.append(write)

    if chunks > 1:
        total[...] = jnp.zeros_like(total)

        def partial(chunk, carry):
            maps_of(chunk, False)
            return carry

        lax.fori_loop(0, chunks - 1, partial, 0)
    maps_of(chunks - 1, True)
    for write in writes:
        write.wait()


def local(blks, dirs, sky_map, order_ids, legendre, wigner, wavelet, dir_ids):
    devices = blks * dirs
    cycles, turn = sky_map.shape[1:]
    orders = legendre.shape[0]
    vmem = pl.BlockSpec(memory_space=pltpu.VMEM)
    hbm = pl.BlockSpec(memory_space=pltpu.HBM)
    slots = jax.ShapeDtypeStruct((2, blks * orders, LANES), jnp.float32)
    sky_map, legendre, wigner, wavelet, order_ids, dir_ids = (pltpu.with_memory_space_constraint(x, pltpu.HBM) for x in (sky_map, legendre, wigner, wavelet, order_ids, dir_ids))
    slab = LANES // cycles * orders
    chunks = blks * orders // slab
    table = jax.ShapeDtypeStruct((chunks * 6 * slab, 2 * INNER), jnp.bfloat16)
    turns = jax.ShapeDtypeStruct((chunks, turn // INNER // 2, 2, slab, LANES), jnp.float32)
    middle = pl.pallas_call(
        functools.partial(spectra_kernel, blks, dirs),
        out_shape=(slots, table, turns),
        in_specs=[hbm] * 6,
        out_specs=(vmem, vmem, vmem),
        scratch_shapes=[
            pltpu.SMEM(order_ids.shape, jnp.int32),
            pltpu.SMEM(dir_ids.shape, jnp.int32),
            pltpu.VMEM(sky_map.shape, jnp.float32),
            pltpu.VMEM(legendre.shape, jnp.float32),
            pltpu.VMEM(wigner.shape, jnp.float32),
            pltpu.VMEM(wavelet.shape, jnp.float32),
            pltpu.VMEM((blks, 1, LANES), jnp.float32),
            pltpu.VMEM((devices, 1, LANES), jnp.float32),
            pltpu.VMEM((blks, orders, LANES), jnp.float32),
            pltpu.VMEM((devices, orders, LANES), jnp.float32),
            pltpu.SemaphoreType.DMA((6,)),
            pltpu.SemaphoreType.DMA((2,)),
            pltpu.SemaphoreType.DMA((2,)),
        ],
        compiler_params=pltpu.CompilerParams(
            collective_id=0, has_side_effects=True, vmem_limit_bytes=48 * 2**20
        ),
    )(order_ids, dir_ids, sky_map, legendre, wigner, wavelet)
    several = chunks > 1
    total_shape = (turn // INNER // 2, LANES, 2 * INNER) if several else (1, 8, LANES)
    out = jax.ShapeDtypeStruct((1, dirs, cycles, turn), jnp.float32)
    return pl.pallas_call(
        functools.partial(maps_kernel, turn, dirs, cycles),
        out_shape=out,
        in_specs=[vmem] * 3,
        out_specs=hbm,
        scratch_shapes=[
            pltpu.VMEM(out.shape, jnp.float32),
            pltpu.VMEM(total_shape, jnp.float32),
            pltpu.SemaphoreType.DMA((turn // INNER // 2,)),
        ],
        compiler_params=pltpu.CompilerParams(vmem_limit_bytes=48 * 2**20),
    )(*middle)


def solution(mesh):
    return jax.shard_map(
        functools.partial(local, mesh.shape["blk"], mesh.shape["dir"]),
        mesh=mesh,
        in_specs=(
            P("dir", "blk", None),
            P(),
            P("blk", None, None),
            P("dir", "blk", None, None),
            P("dir", None),
            P(),
        ),
        out_specs=P("dir", None, "blk", None),
        check_vma=False,
    )
```
